32 devices in a mesh: ctx: 8 (over z, x), tp: 4 (over y, core).
Axes of the slice: x: 2, y: 2, z: 4, core: 2. Of those that a mesh axis runs over, the one named last changes fastest.
Arguments:
- hidden_states: bfloat16 [768, 8192], P('ctx', 'tp'), may hold values from -6 to 6
- counts: int32 [8], P('ctx'), may hold values from 24 to 72, as said below
- selected: int32 [8, 72], P('ctx'), may hold values from 0 to 95, as said below
- router_weight: float32 [768], P('ctx'), may hold values from 0.25 to 1.5
- norm_gain: float32 [8192], P('tp'), may hold values from 0.25 to 1.75
- w_gate: bfloat16 [8192, 28672], P('tp', 'ctx'), may hold values from -0.0625 to 0.0625
- w_up: bfloat16 [8192, 28672], P('tp', 'ctx'), may hold values from -0.0625 to 0.0625
- w_down: bfloat16 [28672, 8192], P('ctx', 'tp'), may hold values from -0.03125 to 0.03125
Outputs:
- block_out: bfloat16 [768, 8192], P('ctx', 'tp')
The draws below stay inside these ranges and needn't reach their ends.
Inputs may be any that keep to these rules, and one draw needn't show every extreme that they name: The counts sum to 384; for every shard s the counts of the shards before s sum to between s * 48 - 48 // 4 and s * 48 + 48 // 4. `selected`: the entries of a row are distinct; only the first counts[s] entries of row s are used.
All inputs are finite; a program needn't handle non-finite values.
Results may differ from the reference program's by a relative error of at most 0.014.
Values may be sent and summed in bfloat16 or wider, within the bound.
No kernel may reach another device: no remote copies, remote signals or barrier semaphores. Data moves between devices by JAX's collectives and lax.ppermute only.
A program may use at most 128 MiB of HBM per device.

```python
import jax
import jax.numpy as jnp
from jax import lax

D = 8192
FF = 28672
TOK_DEV = 96
SEL = 48
MAXSEL = 72
TOKENS = 768
N_CTX = 8


def draw_counts(key, part):
    quarter = SEL // 4
    first_key = jax.random.fold_in(key, 11)
    second_key = jax.random.fold_in(key, 12)
    excess = jax.random.randint(first_key, (N_CTX,), -quarter, quarter + 1).astype(jnp.int32)
    positions = jnp.arange(N_CTX, dtype=jnp.int32)
    excess = jnp.where(positions == N_CTX - 1, 0, excess)
    heavy = jax.random.randint(second_key, (), 1, N_CTX - 1).astype(jnp.int32)
    excess = jnp.where(positions == heavy, quarter, excess)
    excess = jnp.where(positions == heavy - 1, -quarter, excess)
    before = jnp.concatenate([jnp.zeros((1,), jnp.int32), excess[:-1]])
    return (SEL + excess - before).astype(jnp.int32)


def draw_selected(key, part):
    subkeys = jax.random.split(jax.random.fold_in(key, 21), N_CTX)
    orders = jax.vmap(lambda single: jax.random.permutation(single, TOK_DEV))(subkeys).astype(jnp.int32)
    leading = orders[:, :1]
    orders = jnp.where(orders == TOK_DEV - 1, leading, orders)
    orders = orders.at[:, 0].set(TOK_DEV - 1)
    return orders[:, :MAXSEL].astype(jnp.int32)


def levels(rng, dims, cuts, low, high):
    loudness, own = 1.0, jax.random.fold_in(rng, 6)
    for position, parts in cuts:
        heights = jnp.exp(jax.random.uniform(jax.random.fold_in(own, position), (parts,), jnp.float32, low / len(cuts), high / len(cuts)))
        loudness = loudness * jnp.repeat(heights, dims[position] // parts).reshape([-1 if axis == position else 1 for axis in range(len(dims))])
    return loudness


def gaussian(key, dims, scale, limit, cuts=(), kind=jnp.bfloat16):
    values = scale * jax.random.normal(key, dims, jnp.float32)
    if cuts:
        values = values * levels(key, dims, cuts, -0.22, 0.18)
    return jnp.clip(values, -limit, limit).astype(kind)


def setup_inputs(seed: int = 0) -> dict:
    splits = jax.random.split(jax.random.key(seed), 9)
    return {
        "hidden_states": gaussian(splits[0], (TOKENS, D), 1.0, 6.0, ((0, 8), (1, 4))),
        "counts": draw_counts(jax.random.fold_in(splits[8], 71), 0),
        "selected": draw_selected(jax.random.fold_in(splits[8], 71), 0),
        "router_weight": jnp.clip(0.25 + 1.25 * jax.random.uniform(splits[3], (TOKENS,), jnp.float32) ** levels(splits[3], (TOKENS,), ((0, 8),), -0.2, 0.2), 0.25, 1.5),
        "norm_gain": jnp.clip(1.0 + 0.15 * jax.random.normal(splits[4], (D,), jnp.float32), 0.25, 1.75),
        "w_gate": gaussian(splits[5], (D, FF), D ** -0.5, 0.0625, ((0, 4), (1, 8))),
        "w_up": gaussian(splits[6], (D, FF), D ** -0.5, 0.0625, ((0, 4), (1, 8))),
        "w_down": gaussian(splits[7], (FF, D), FF ** -0.5, 0.03125, ((0, 8), (1, 4))),
    }


def reference(hidden_states, counts, selected, router_weight, norm_gain, w_gate, w_up, w_down):
    shards = hidden_states.reshape(N_CTX, TOK_DEV, D)
    picked = jnp.take_along_axis(shards, selected[:, :, None].astype(jnp.int32), axis=1).astype(jnp.float32)
    mean_sq = lax.optimization_barrier(jnp.mean(picked * picked, axis=-1, keepdims=True))
    normed = (picked * lax.rsqrt(mean_sq + 1e-05) * norm_gain.astype(jnp.float32)).astype(jnp.bfloat16)
    normed = normed.reshape(N_CTX * MAXSEL, D)
    gate = jnp.dot(normed, w_gate, preferred_element_type=jnp.float32)
    up_part = jnp.dot(normed, w_up, preferred_element_type=jnp.float32)
    hidden = (jax.nn.silu(gate) * up_part).astype(jnp.bfloat16)
    width = FF // N_CTX
    total = jnp.zeros((N_CTX * MAXSEL, D), jnp.float32)
    for group in range(N_CTX):
        partial_sum = jnp.dot(hidden[:, group * width:(group + 1) * width], w_down[group * width:(group + 1) * width], preferred_element_type=jnp.float32)
        total = total + partial_sum.astype(jnp.bfloat16).astype(jnp.float32)
    ffn_rows = lax.optimization_barrier(total.astype(jnp.bfloat16)).astype(jnp.float32)
    ffn_rows = ffn_rows.reshape(N_CTX, MAXSEL, D)
    active = (jnp.arange(MAXSEL, dtype=jnp.int32)[None, :] < counts[:, None]).astype(jnp.float32)
    weights = jnp.take_along_axis(router_weight.reshape(N_CTX, TOK_DEV), selected.astype(jnp.int32), axis=1).astype(jnp.float32) * active
    delta = ffn_rows * weights[:, :, None]
    onehot = (jnp.arange(TOK_DEV, dtype=jnp.int32)[None, :, None] == selected[:, None, :]).astype(jnp.float32)
    added = jnp.einsum('ntm,nmd->ntd', onehot, delta, precision=lax.Precision.HIGHEST)
    result = (shards.astype(jnp.float32) + added).astype(jnp.bfloat16)
    return result.reshape(N_CTX * TOK_DEV, D)
```

```python
import functools

import jax
import jax.numpy as jnp
from jax import lax
from jax.experimental import pallas as pl
from jax.experimental.pallas import tpu as pltpu
from jax.sharding import PartitionSpec as P

D = 8192
SEL = 48
SURE = SEL // 2
SLACK = SEL // 4
GROUP = 4
EPS = 1e-05
MIB = 1 << 20
F32 = jnp.float32
BF16 = jnp.bfloat16


def swap(value, axis, size, bit):
    return lax.ppermute(value, axis, [(i, i ^ bit) for i in range(size)])


def gate_up_kernel(me_ref, x_ref, g_ref, u_ref, send_ref, keep_ref):
    width = g_ref.shape[1]

    def fill(out):
        x = x_ref[...]
        out[0, :, :width] = jnp.dot(x, g_ref[...], preferred_element_type=F32).astype(BF16)
        out[0, :, width:] = jnp.dot(x, u_ref[...], preferred_element_type=F32).astype(BF16)

    @pl.when(pl.program_id(0) == 0)
    def _():
        fill(send_ref)

    @pl.when(pl.program_id(0) == 1)
    def _():
        fill(keep_ref)


def gate_up(me, x, w_gate, w_up, tp):
    rows, feats = x.shape
    units = w_gate.shape[1]
    width = units // tp
    if width % 128:
        sums = [
            jnp.dot(x, w, preferred_element_type=F32).astype(BF16).reshape(rows, tp, width)
            for w in (w_gate, w_up)
        ]
        shares = jnp.concatenate(sums, axis=2).transpose(1, 0, 2)
        send, keep = (shares[(me[0] ^ k) ^ jnp.array([2, 0])] for k in (1, 0))
        return send, keep
    weight = pl.BlockSpec(
        (feats, width), lambda k, h, me: (0, me[0] ^ (1 - k) ^ (2 * (1 - h)))
    )
    half = jax.ShapeDtypeStruct((2, rows, 2 * width), BF16)
    return pl.pallas_call(
        gate_up_kernel,
        out_shape=(half, half),
        grid_spec=pltpu.PrefetchScalarGridSpec(
            num_scalar_prefetch=1,
            grid=(2, 2),
            in_specs=[pl.BlockSpec((rows, feats), lambda k, h, me: (0, 0)), weight, weight],
            out_specs=[
                pl.BlockSpec((1, rows, 2 * width), lambda k, h, me: (jnp.where(k == 0, h, 1), 0, 0)),
                pl.BlockSpec((1, rows, 2 * width), lambda k, h, me: (jnp.where(k == 0, 0, h), 0, 0)),
            ],
        ),
        compiler_params=pltpu.CompilerParams(vmem_limit_bytes=28 * MIB),
        cost_estimate=pl.CostEstimate(
            flops=4 * rows * feats * units, bytes_accessed=4 * feats * units, transcendentals=0
        ),
        name=f"gate_up_{rows}",
    )(me, x, w_gate, w_up)


def down_kernel(me_ref, h0, h1, h2, h3, w_ref, out_ref, acc):
    step = pl.program_id(0)
    for position, hidden in enumerate((h0, h1, h2, h3)):

        @pl.when(step == position)
        def _():
            term = jnp.dot(hidden[...], w_ref[...], preferred_element_type=F32)
            if position == 0:
                acc[...] = term
            elif position < 3:
                acc[...] += term
            else:
                out_ref[...] = (acc[...] + term).astype(BF16)


def down(me, hiddens, w_down):
    rows, width = hiddens[0].shape
    units, feats = w_down.shape
    whole = pl.BlockSpec((rows, width), lambda j, me: (0, 0))
    return pl.pallas_call(
        down_kernel,
        out_shape=jax.ShapeDtypeStruct((rows, feats), BF16),
        grid_spec=pltpu.PrefetchScalarGridSpec(
            num_scalar_prefetch=1,
            grid=(4,),
            in_specs=[whole] * 4
            + [pl.BlockSpec((width, feats), lambda j, me: (me[0] ^ (j // 2) ^ (2 * (j % 2)), 0))],
            out_specs=pl.BlockSpec((rows, feats), lambda j, me: (0, 0)),
            scratch_shapes=[pltpu.VMEM((rows, feats), F32)],
        ),
        compiler_params=pltpu.CompilerParams(vmem_limit_bytes=20 * MIB),
        cost_estimate=pl.CostEstimate(
            flops=2 * rows * feats * units, bytes_accessed=2 * feats * units, transcendentals=0
        ),
        name=f"down_{rows}",
    )(me, *hiddens, w_down)


def feed_forward(me, tp, x, gain, w_gate, w_up, w_down):
    xf = x.astype(F32)
    squares = jnp.sum(xf * xf, axis=-1)
    scaled = (xf * gain[None, :]).astype(BF16)
    send, keep = gate_up(me, scaled, w_gate, w_up, tp)
    squares = squares + swap(squares, "tp", tp, 1)
    got = swap(send, "tp", tp, 1)
    squares = squares + swap(squares, "tp", tp, 2)
    outgoing = (keep[0].astype(F32) + got[0].astype(F32)).astype(BF16)
    across = swap(outgoing, "tp", tp, 2)
    total = keep[1].astype(F32) + got[1].astype(F32) + across.astype(F32)
    total = total * lax.rsqrt(squares / D + EPS)[:, None]
    width = total.shape[1] // 2
    gate, up = total[:, :width], total[:, width:]
    own = (jax.nn.silu(gate) * up).astype(BF16)
    other_y = swap(own, "tp", tp, 2)
    other_core = swap(own, "tp", tp, 1)
    both = swap(other_y, "tp", tp, 1)
    return down(me, (own, other_y, other_core, both), w_down)


def gather_group(rows, n_ctx):
    return [rows] + [swap(rows, "ctx", n_ctx, j) for j in range(1, GROUP)]


def reduce_group(blocks, n_ctx):
    total = blocks[0].astype(F32)
    for j in range(1, GROUP):
        total = total + swap(blocks[j], "ctx", n_ctx, j).astype(F32)
    return total


def packing(extras, slots, window):
    starts = jnp.cumsum(extras) - extras
    slot = jnp.arange(slots, dtype=jnp.int32)[:, None, None]
    row = jnp.arange(window, dtype=jnp.int32)[None, None, :]
    hit = (slot == starts[None, :, None] + row) & (row < extras[None, :, None])
    return hit.astype(BF16).reshape(slots, GROUP * window)


def body(hidden_states, counts, selected, router_weight, norm_gain, w_gate, w_up, w_down, *, n_ctx, tp):
    me = lax.axis_index("tp").astype(jnp.int32).reshape(1)
    chosen = selected[0]
    count = counts[0]
    most = chosen.shape[0]
    tokens, feats = hidden_states.shape
    window = most - SURE
    payload = most + 8
    inner = min(2, n_ctx // GROUP - 1)
    slots = -(-(GROUP * (SEL - SURE) + SLACK * inner) // 16) * 16

    index = jnp.arange(payload, dtype=jnp.int32)
    listed = jnp.concatenate([chosen, jnp.zeros((payload - most,), jnp.int32)])
    active = (index < most) & (index < count)
    place = jnp.arange(tokens, dtype=jnp.int32)
    pick = ((listed[:, None] == place[None, :]) & active[:, None]).astype(BF16)
    rows = jnp.dot(pick, hidden_states, preferred_element_type=F32)
    rows = jnp.where((index == most)[:, None], count.astype(F32), rows).astype(BF16)
    sure, rest = rows[:SURE], rows[SURE:]

    def unpack(members):
        extras = jnp.stack([m[most - SURE, 0] for m in members]).astype(jnp.int32) - SURE
        map_ = packing(extras, slots, window)
        stacked = jnp.concatenate([m[:window] for m in members])
        return jnp.dot(map_, stacked, preferred_element_type=F32).astype(BF16), map_

    def spread(map_, partial):
        wide = jnp.dot(map_.T, partial, preferred_element_type=F32).astype(BF16)
        return [wide[j * window : (j + 1) * window] for j in range(GROUP)]

    def split(partial):
        return [partial[j * SURE : (j + 1) * SURE] for j in range(GROUP)]

    run = functools.partial(
        feed_forward, me, tp, gain=norm_gain, w_gate=w_gate, w_up=w_up, w_down=w_down
    )
    near_sure = jnp.concatenate(gather_group(sure, n_ctx))
    far_rows = [swap(rows, "ctx", n_ctx, d) for d in range(GROUP, n_ctx, GROUP)]
    near_rest, near_map = unpack(gather_group(rest, n_ctx))

    total_sure = reduce_group(split(run(near_sure)), n_ctx)
    total_rest = 0.0
    for number, mine in enumerate(far_rows):
        members = gather_group(mine, n_ctx)
        far_sure = jnp.concatenate([m[:SURE] for m in members])
        far_rest, far_map = unpack([m[SURE:] for m in members])
        partial = run(jnp.concatenate([far_sure, far_rest]))
        blocks = [
            jnp.concatenate(pair)
            for pair in zip(split(partial[: GROUP * SURE]), spread(far_map, partial[GROUP * SURE :]))
        ]
        summed = reduce_group(blocks, n_ctx).astype(BF16)
        back = swap(summed, "ctx", n_ctx, GROUP * (number + 1)).astype(F32)
        total_sure = total_sure + back[:SURE]
        total_rest = total_rest + back[SURE:]
    total_rest = total_rest + reduce_group(spread(near_map, run(near_rest)), n_ctx)

    ffn = jnp.concatenate([total_sure, total_rest]).astype(BF16)
    put = ((chosen[None, :] == place[:, None]) & active[None, :most]).astype(BF16)
    added = jnp.dot(put, ffn, preferred_element_type=F32) * router_weight[:, None]
    return (hidden_states.astype(F32) + added).astype(BF16)


def solution(mesh):
    placed = (
        P("ctx", "tp"),
        P("ctx"),
        P("ctx", None),
        P("ctx"),
        P("tp"),
        P("tp", "ctx"),
        P("tp", "ctx"),
        P("ctx", "tp"),
    )
    return jax.shard_map(
        functools.partial(body, n_ctx=mesh.shape["ctx"], tp=mesh.shape["tp"]),
        mesh=mesh,
        in_specs=placed,
        out_specs=P("ctx", "tp"),
        check_vma=False,
    )
```

```python
import functools

import jax
import jax.numpy as jnp
from jax import lax
from jax.experimental import pallas as pl
from jax.experimental.pallas import tpu as pltpu
from jax.sharding import PartitionSpec as P

D = 8192
SEL = 48
SURE = SEL // 2
SLACK = SEL // 4
GROUP = 4
EPS = 1e-05
NONE = 1024.0
MIB = 1 << 20
LANES = 256
SPARE = 3
F32 = jnp.float32
BF16 = jnp.bfloat16
VMEM = pl.BlockSpec(memory_space=pltpu.VMEM)
SMEM = pl.BlockSpec(memory_space=pltpu.SMEM)
HBM = pl.BlockSpec(memory_space=pltpu.HBM)
ANY = pl.BlockSpec(memory_space=pl.ANY)


def swap(value, axis, size, bit):
    return lax.ppermute(value, axis, [(i, i ^ bit) for i in range(size)])


def call(kernel, outs, operands, specs, name, limit, scratch=(), after=()):
    made = pl.pallas_call(
        kernel,
        out_shape=[jax.ShapeDtypeStruct(shape, dtype) for shape, dtype in outs],
        in_specs=list(specs) + [ANY] * len(after),
        out_specs=[VMEM] * len(outs),
        scratch_shapes=list(scratch),
        compiler_params=pltpu.CompilerParams(vmem_limit_bytes=limit * MIB),
        name=name,
    )(*operands, *after)
    return list(made)


def pick_kernel(count_ref, chosen_ref, tokens_ref, out_ref):
    tokens, most = tokens_ref.shape[0], out_ref.shape[0]
    place = lax.broadcasted_iota(jnp.int32, (tokens, most), 0)
    rows = lax.dot_general(
        jnp.where(chosen_ref[...] == place, 1.0, 0.0).astype(BF16),
        tokens_ref[...],
        (((0,), (0,)), ((), ())),
        preferred_element_type=F32,
    )
    index = lax.broadcasted_iota(jnp.int32, rows.shape, 0)
    out_ref[...] = jnp.where(index < count_ref[0], rows, NONE).astype(BF16)


def slots_of(index, extras, start, member, window):
    index = index.astype(F32)
    in_rest = index - SURE
    slot = jnp.where(index < SURE, index + member * SURE, in_rest + start + GROUP * SURE)
    valid = (index < SURE) | ((in_rest < extras) & (in_rest < window))
    return jnp.where(valid, slot, -1.0)


def assemble_kernel(gain_ref, *refs, window):
    sources, (x_ref, squares_ref, extras_ref) = refs[:GROUP], refs[-3:]
    rows, feats = x_ref.shape
    payload = sources[0].shape[0]
    lanes = extras_ref.shape[1]
    total = jnp.zeros((rows, feats), F32)
    start = jnp.zeros((1, lanes), F32)
    extras_ref[...] = jnp.zeros_like(extras_ref)
    for member, source in enumerate(sources):
        marks = source[:, :lanes].astype(F32)
        extras = jnp.sum(jnp.where(marks < NONE, 1.0, 0.0), axis=0, keepdims=True) - SURE
        extras_ref[member : member + 1, :] = extras
        index = lax.broadcasted_iota(jnp.int32, (rows, payload), 1)
        slot = slots_of(index, extras[:, :payload], start[:, :payload], member, window)
        here = lax.broadcasted_iota(jnp.int32, (rows, payload), 0).astype(F32)
        hit = jnp.where(slot == here, 1.0, 0.0).astype(BF16)
        total += jnp.dot(hit, source[...], preferred_element_type=F32)
        start = start + extras
    x_ref[...] = (total * gain_ref[...]).astype(BF16)
    sums = jnp.sum(total * total, axis=1, keepdims=True)
    row = lax.broadcasted_iota(jnp.int32, (rows, lanes), 0)
    lane = lax.broadcasted_iota(jnp.int32, (rows, lanes), 1)
    spread = jnp.sum(jnp.where(row == lane, sums, 0.0), axis=0, keepdims=True)
    squares_ref[...] = jnp.broadcast_to(spread, squares_ref.shape)


def assemble(gain, sources, rows, window, after=()):
    feats = sources[0].shape[1]
    return call(
        functools.partial(assemble_kernel, window=window),
        [((rows, feats), BF16), ((8, LANES), F32), ((8, LANES), F32)],
        (gain, *sources),
        [VMEM] * (1 + GROUP),
        f"assemble_{rows}",
        24,
        after=after,
    )


def coded(squares, block):
    high = squares.astype(BF16).astype(F32)
    middle = (squares - high).astype(BF16).astype(F32)
    width = block.shape[1]
    terms = []
    for term in (high, middle, squares - high - middle):
        if width > LANES:
            term = jnp.concatenate([term, jnp.zeros((1, width - LANES), F32)], axis=1)
        terms.append(term[:, :width])
    row = lax.broadcasted_iota(jnp.int32, block.shape, 0) - (block.shape[0] - SPARE)
    block = block.astype(F32)
    for number, term in enumerate(terms):
        block = jnp.where(row == number, term, block)
    return block.astype(BF16)


def decoded(block):
    block = block.astype(F32)
    total = block[13:14] + block[14:15] + block[15:16]
    if total.shape[1] < LANES:
        total = jnp.concatenate([total, jnp.zeros((1, LANES - total.shape[1]), F32)], axis=1)
    return total[:, :LANES]


def gate_up_kernel(me_ref, x_ref, s_ref, g_ref, u_ref, *refs, share_width, cuts, shares, count):
    outs, (buffer, sems) = refs[-2 - count : -2], refs[-2:]
    me = me_ref[0]
    rows = x_ref.shape[0]
    slots = buffer.shape[0]
    tiles = [(step, array, cut) for step in range(2) for array in range(2) for cut in range(len(cuts))]

    def copy(tile):
        step, array, cut = tiles[tile]
        offset, width = cuts[cut]
        begin = pl.multiple_of((me ^ shares[step]) * share_width + offset, 128)
        source = (g_ref, u_ref)[array].at[:, pl.ds(begin, width)]
        slot = tile % slots
        return pltpu.make_async_copy(source, buffer.at[slot, :, pl.ds(0, width)], sems.at[slot])

    for tile in range(min(slots, len(tiles))):
        copy(tile).start()
    for tile, (step, array, cut) in enumerate(tiles):
        offset, width = cuts[cut]
        copy(tile).wait()
        term = jnp.dot(x_ref[...], buffer[tile % slots, :, :width], preferred_element_type=F32)
        if tile + slots < len(tiles):
            copy(tile + slots).start()
        if step == 1 or count == 2:
            place = pl.ds(array * share_width + offset, width)
            outs[step - 2][:, place] = term.astype(BF16)
        elif tile == 0:
            outs[0][: rows - 16, :] = term[: rows - 16].astype(BF16)
            outs[0][rows - 16 :, :] = coded(s_ref[0:1, :], term[rows - 16 :])
        else:
            outs[tile][...] = term.astype(BF16)


def gate_up(me, x, squares, w_gate, w_up, tp, cuts, mine, after):
    rows, feats = x.shape
    width = w_gate.shape[1] // tp
    shares = (1, 0) if mine else (3, 2)
    if width % 128:
        sums = [
            jnp.dot(x, w, preferred_element_type=F32).astype(BF16).reshape(rows, tp, width)
            for w in (w_gate, w_up)
        ]
        out = [
            [lax.dynamic_index_in_dim(p, me[0] ^ share, 1, False) for p in sums] for share in shares
        ]
        joined = [jnp.concatenate(pair, axis=1) for pair in out]
        if mine:
            return joined
        return [coded(squares[0:1], out[0][0]), out[0][1], joined[1]]
    whole = ((rows, 2 * width), BF16)
    pieces = [((rows, w), BF16) for _ in range(2) for _, w in cuts]
    outs = [whole] * 2 if mine else pieces + [whole]
    return call(
        functools.partial(
            gate_up_kernel, share_width=width, cuts=cuts, shares=shares, count=len(outs)
        ),
        outs,
        (me, x, squares, w_gate, w_up),
        [SMEM, VMEM, VMEM, HBM, HBM],
        f"gate_up_{rows}_{int(mine)}",
        50,
        scratch=[
            pltpu.VMEM((4, feats, max(w for _, w in cuts)), BF16),
            pltpu.SemaphoreType.DMA((4,)),
        ],
        after=after,
    )


def add_kernel(own_ref, s_ref, *refs, cuts, count):
    gots, (out_ref, sum_ref) = refs[:count], refs[-2:]
    rows, width = own_ref.shape
    for number, got in enumerate(gots):
        array, cut = divmod(number, len(cuts))
        offset, part = cuts[cut]
        place = pl.ds(array * (width // 2) + offset, part)
        total = own_ref[:, place].astype(F32) + got[...].astype(F32)
        out_ref[:, place] = total.astype(BF16)
    squares = s_ref[0:1, :] + decoded(gots[0][rows - 16 :, :])
    out_ref[rows - 16 :, :] = coded(squares, out_ref[rows - 16 :, :])
    sum_ref[...] = jnp.broadcast_to(squares, sum_ref.shape)


def add(own, gots, squares, cuts, after):
    return call(
        functools.partial(add_kernel, cuts=cuts, count=len(gots)),
        [(own.shape, BF16), ((8, LANES), F32)],
        (own, squares, *gots),
        [VMEM] * (2 + len(gots)),
        "add",
        16,
        after=after,
    )


def silu_kernel(a_ref, b_ref, c_ref, s_ref, *refs):
    out_ref = refs[-1]
    rows, width = out_ref.shape
    squares = s_ref[0:1, :] + decoded(c_ref[rows - 16 :, :])
    row = lax.broadcasted_iota(jnp.int32, (rows, LANES), 0)
    lane = lax.broadcasted_iota(jnp.int32, (rows, LANES), 1)
    column = jnp.sum(jnp.where(row == lane, squares, 0.0), axis=1, keepdims=True)
    scale = jnp.where(row[:, :1] < rows - SPARE, lax.rsqrt(column / D + EPS), 0.0)

    def total(part):
        return (
            a_ref[:, part].astype(F32) + b_ref[:, part].astype(F32) + c_ref[:, part].astype(F32)
        ) * scale

    gate, up = total(slice(0, width)), total(slice(width, 2 * width))
    out_ref[...] = (gate / (1.0 + jnp.exp(-gate)) * up).astype(BF16)


def silu(a, b, c, squares, after):
    rows, width = a.shape
    return call(
        silu_kernel,
        [((rows, width // 2), BF16)],
        (a, b, c, squares),
        [VMEM] * 4,
        "silu",
        16,
        after=after,
    )[0]


def relay_kernel(in_ref, *refs):
    refs[-1][...] = in_ref[...]


def relay(value, after):
    return call(relay_kernel, [(value.shape, value.dtype)], (value,), [VMEM], "relay", 16, after=after)[0]


def down_kernel(me_ref, extras_ref, h0, h1, w_ref, *refs, shares, parts, window, last):
    outs, (acc, buffer, sems) = refs[-GROUP - 3 if last else -4 : -3], refs[-3:]
    me = me_ref[0]
    width = h0.shape[1]
    depth = width // parts
    tiles = [(number, part) for number in range(2) for part in range(parts)]

    def copy(tile):
        number, part = tiles[tile]
        begin = pl.multiple_of((me ^ shares[number]) * width + part * depth, 16)
        return pltpu.make_async_copy(w_ref.at[pl.ds(begin, depth), :], buffer.at[tile], sems.at[tile])

    for tile in range(len(tiles)):
        copy(tile).start()
    for tile, (number, part) in enumerate(tiles):
        copy(tile).wait()
        hidden = (h0, h1)[number][:, part * depth : (part + 1) * depth]
        term = jnp.dot(hidden, buffer[tile], preferred_element_type=F32)
        if tile == 0:
            acc[...] = refs[0][...] + term if last else term
        else:
            acc[...] += term
    if not last:
        outs[0][...] = acc[...]
        return

    partial = acc[...].astype(BF16)
    rows = partial.shape[0]
    start = jnp.zeros((1, extras_ref.shape[1]), F32)
    for member, out in enumerate(outs):
        extras = extras_ref[member : member + 1, :]
        index = lax.broadcasted_iota(jnp.int32, (out.shape[0], rows), 0)
        slot = slots_of(index, extras[:, :rows], start[:, :rows], member, window)
        here = lax.broadcasted_iota(jnp.int32, (out.shape[0], rows), 1).astype(F32)
        hit = jnp.where(slot == here, 1.0, 0.0).astype(BF16)
        out[...] = jnp.dot(hit, partial, preferred_element_type=F32).astype(BF16)
        start = start + extras


def down(me, extras, w_down, hiddens, before, window, after):
    rows, width = hiddens[0].shape
    feats = w_down.shape[1]
    last = before is not None
    parts = 2 if width % 32 == 0 else 1
    return call(
        functools.partial(
            down_kernel, shares=(2, 3) if last else (0, 1), parts=parts, window=window, last=last
        ),
        [((SURE + window, feats), BF16)] * GROUP if last else [((rows, feats), F32)],
        (me, extras, *hiddens, w_down) + ((before,) if last else ()),
        [SMEM, VMEM, VMEM, VMEM, HBM] + [VMEM] * last,
        f"down_{rows}_{int(last)}",
        50,
        scratch=[
            pltpu.VMEM((rows, feats), F32),
            pltpu.VMEM((2 * parts, width // parts, feats), BF16),
            pltpu.SemaphoreType.DMA((2 * parts,)),
        ],
        after=after,
    )


def gather_group(rows, n_ctx):
    return [rows] + [swap(rows, "ctx", n_ctx, j) for j in range(1, GROUP)]


def sum_kernel(a_ref, b_ref, c_ref, d_ref, *refs):
    total = a_ref[...].astype(F32) + b_ref[...].astype(F32)
    refs[-1][...] = (total + c_ref[...].astype(F32) + d_ref[...].astype(F32)).astype(BF16)


def reduce_group(blocks, n_ctx, after):
    got = [blocks[0]] + [swap(blocks[j], "ctx", n_ctx, j) for j in range(1, GROUP)]
    return call(
        sum_kernel, [(blocks[0].shape, BF16)], got, [VMEM] * GROUP, "sum", 16, after=after
    )[0]


def body(hidden_states, counts, selected, router_weight, norm_gain, w_gate, w_up, w_down, *, n_ctx, tp):
    me = lax.axis_index("tp").astype(jnp.int32).reshape(1)
    chosen = selected[0]
    most = chosen.shape[0]
    tokens, feats = hidden_states.shape
    window = most - SURE
    inner = min(2, n_ctx // GROUP - 1)
    slots = -(-(GROUP * (SEL - SURE) + SLACK * inner + SPARE) // 16) * 16
    height = GROUP * SURE + slots
    gain = norm_gain[None, :]
    share_width = w_gate.shape[1] // tp
    first = -(-share_width // 256) * 128
    cuts = [(0, share_width)]
    if share_width % 128 == 0 and first < share_width:
        cuts = [(0, first), (first, share_width - first)]

    rows = call(
        pick_kernel,
        [((most, feats), BF16)],
        (counts, selected, hidden_states),
        [SMEM, VMEM, VMEM],
        "pick",
        16,
    )[0]
    sources = [gather_group(rows, n_ctx)]
    for d in range(GROUP, n_ctx, GROUP):
        sources.append(gather_group(swap(rows, "ctx", n_ctx, d), n_ctx))
    weights = (w_gate, w_up, tp, cuts)

    chunks = [assemble(gain, members, height, window) for members in sources]
    begun, after = [], []
    for number, (x, squares, _) in enumerate(chunks):
        *sends, keep = gate_up(me, x, squares, *weights, False, after)
        gots = [swap(piece, "tp", tp, 1) for piece in sends]
        outgoing, two = add(keep, gots, squares, cuts, [] if number else chunks[1][:1])
        begun.append((swap(outgoing, "tp", tp, 2), two))
        after = [outgoing]
    owns, cores, parts = [], [], []
    for (x, squares, extras), (across, two) in zip(chunks, begun):
        send, keep = gate_up(me, x, squares, *weights, True, after)
        own = silu(keep, swap(send, "tp", tp, 1), across, two, parts[:1])
        after = [own]
        owns.append(own)
        cores.append(swap(own, "tp", tp, 1))
        if not parts:
            parts.append(down(me, extras, w_down, (own, cores[0]), None, window, [])[0])

    blocks, behind = [], []
    for number in [*range(1, len(chunks)), 0]:
        extras = chunks[number][2]
        other_y = swap(owns[number], "tp", tp, 2)
        if number:
            hidden = (owns[number], cores[number])
            part = down(me, extras, w_down, hidden, None, window, behind)[0]
        else:
            part = parts[0]
        other_y = relay(other_y, [part] + behind)
        both = swap(other_y, "tp", tp, 1)
        blocks.append(down(me, extras, w_down, (other_y, both), part, window, []))
        behind = blocks[-1][:1]

    total = 0.0
    for number, parts in enumerate(blocks[:-1]):
        summed = reduce_group(parts, n_ctx, blocks[-1][:1])
        total = total + swap(summed, "ctx", n_ctx, GROUP * (number + 1)).astype(F32)
    for number, part in enumerate(blocks[-1]):
        total = total + (swap(part, "ctx", n_ctx, number) if number else part).astype(F32)

    ffn = total.astype(BF16)
    active = jnp.arange(most, dtype=jnp.int32) < counts[0]
    place = jnp.arange(tokens, dtype=jnp.int32)
    put = ((chosen[None, :] == place[:, None]) & active[None, :]).astype(BF16)
    added = jnp.dot(put, ffn, preferred_element_type=F32) * router_weight[:, None]
    return (hidden_states.astype(F32) + added).astype(BF16)


def solution(mesh):
    placed = (
        P("ctx", "tp"),
        P("ctx"),
        P("ctx", None),
        P("ctx"),
        P("tp"),
        P("tp", "ctx"),
        P("tp", "ctx"),
        P("ctx", "tp"),
    )
    return jax.shard_map(
        functools.partial(body, n_ctx=mesh.shape["ctx"], tp=mesh.shape["tp"]),
        mesh=mesh,
        in_specs=placed,
        out_specs=P("ctx", "tp"),
        check_vma=False,
    )
```

```python
import functools

import jax
import jax.numpy as jnp
from jax import lax
from jax.experimental import pallas as pl
from jax.experimental.pallas import tpu as pltpu
from jax.sharding import PartitionSpec as P

D = 8192
SEL = 48
SURE = SEL // 2
SLACK = SEL // 4
GROUP = 4
EPS = 1e-05
NONE = 1024.0
MIB = 1 << 20
LANES = 256
SPARE = 3
F32 = jnp.float32
BF16 = jnp.bfloat16
VMEM = pl.BlockSpec(memory_space=pltpu.VMEM)
SMEM = pl.BlockSpec(memory_space=pltpu.SMEM)
HBM = pl.BlockSpec(memory_space=pltpu.HBM)
ANY = pl.BlockSpec(memory_space=pl.ANY)


def swap(value, axis, size, bit):
    return lax.ppermute(value, axis, [(i, i ^ bit) for i in range(size)])


def call(kernel, outs, operands, specs, name, limit, scratch=(), after=()):
    made = pl.pallas_call(
        kernel,
        out_shape=[
            jax.ShapeDtypeStruct(*out) if isinstance(out, tuple) else out for out in outs
        ],
        in_specs=list(specs) + [ANY] * len(after),
        out_specs=[VMEM] * len(outs),
        scratch_shapes=list(scratch),
        compiler_params=pltpu.CompilerParams(vmem_limit_bytes=limit * MIB),
        name=name,
    )(*operands, *after)
    return list(made)


def pick_kernel(count_ref, chosen_ref, tokens_ref, out_ref):
    tokens, most = tokens_ref.shape[0], out_ref.shape[0]
    place = lax.broadcasted_iota(jnp.int32, (tokens, most), 0)
    rows = lax.dot_general(
        jnp.where(chosen_ref[...] == place, 1.0, 0.0).astype(BF16),
        tokens_ref[...],
        (((0,), (0,)), ((), ())),
        preferred_element_type=F32,
    )
    index = lax.broadcasted_iota(jnp.int32, rows.shape, 0)
    out_ref[...] = jnp.where(index < count_ref[0], rows, NONE).astype(BF16)


def slots_of(index, extras, start, member, window):
    index = index.astype(F32)
    in_rest = index - SURE
    slot = jnp.where(index < SURE, index + member * SURE, in_rest + start + GROUP * SURE)
    valid = (index < SURE) | ((in_rest < extras) & (in_rest < window))
    return jnp.where(valid, slot, -1.0)


def assemble_kernel(gain_ref, *refs, window):
    sources, (x_ref, squares_ref, extras_ref) = refs[:GROUP], refs[-3:]
    rows, feats = x_ref.shape
    payload = sources[0].shape[0]
    lanes = extras_ref.shape[1]
    total = jnp.zeros((rows, feats), F32)
    start = jnp.zeros((1, lanes), F32)
    extras_ref[...] = jnp.zeros_like(extras_ref)
    for member, source in enumerate(sources):
        marks = source[:, :lanes].astype(F32)
        extras = jnp.sum(jnp.where(marks < NONE, 1.0, 0.0), axis=0, keepdims=True) - SURE
        extras_ref[member : member + 1, :] = extras
        index = lax.broadcasted_iota(jnp.int32, (rows, payload), 1)
        slot = slots_of(index, extras[:, :payload], start[:, :payload], member, window)
        here = lax.broadcasted_iota(jnp.int32, (rows, payload), 0).astype(F32)
        hit = jnp.where(slot == here, 1.0, 0.0).astype(BF16)
        total += jnp.dot(hit, source[...], preferred_element_type=F32)
        start = start + extras
    x_ref[...] = (total * gain_ref[...]).astype(BF16)
    sums = jnp.sum(total * total, axis=1, keepdims=True)
    row = lax.broadcasted_iota(jnp.int32, (rows, lanes), 0)
    lane = lax.broadcasted_iota(jnp.int32, (rows, lanes), 1)
    spread = jnp.sum(jnp.where(row == lane, sums, 0.0), axis=0, keepdims=True)
    squares_ref[...] = jnp.broadcast_to(spread, squares_ref.shape)


def assemble(gain, sources, rows, window, after=()):
    feats = sources[0].shape[1]
    return call(
        functools.partial(assemble_kernel, window=window),
        [((rows, feats), BF16), ((8, LANES), F32), ((8, LANES), F32)],
        (gain, *sources),
        [VMEM] * (1 + GROUP),
        f"assemble_{rows}",
        24,
        after=after,
    )


def coded(squares, block):
    high = squares.astype(BF16).astype(F32)
    middle = (squares - high).astype(BF16).astype(F32)
    width = block.shape[1]
    terms = []
    for term in (high, middle, squares - high - middle):
        if width > LANES:
            term = jnp.concatenate([term, jnp.zeros((1, width - LANES), F32)], axis=1)
        terms.append(term[:, :width])
    row = lax.broadcasted_iota(jnp.int32, block.shape, 0) - (block.shape[0] - SPARE)
    block = block.astype(F32)
    for number, term in enumerate(terms):
        block = jnp.where(row == number, term, block)
    return block.astype(BF16)


def decoded(block):
    block = block.astype(F32)
    total = block[13:14] + block[14:15] + block[15:16]
    if total.shape[1] < LANES:
        total = jnp.concatenate([total, jnp.zeros((1, LANES - total.shape[1]), F32)], axis=1)
    return total[:, :LANES]


def gate_up_kernel(me_ref, x_ref, s_ref, g_ref, u_ref, *refs, share_width, cuts, shares, count):
    outs, (buffer, sems) = refs[-2 - count : -2], refs[-2:]
    me = me_ref[0]
    rows = x_ref.shape[0]
    slots = buffer.shape[0]
    tiles = [(step, array, cut) for step in range(2) for array in range(2) for cut in range(len(cuts))]

    def copy(tile):
        step, array, cut = tiles[tile]
        offset, width = cuts[cut]
        begin = pl.multiple_of((me ^ shares[step]) * share_width + offset, 128)
        source = (g_ref, u_ref)[array].at[:, pl.ds(begin, width)]
        slot = tile % slots
        return pltpu.make_async_copy(source, buffer.at[slot, :, pl.ds(0, width)], sems.at[slot])

    for tile in range(min(slots, len(tiles))):
        copy(tile).start()
    for tile, (step, array, cut) in enumerate(tiles):
        offset, width = cuts[cut]
        copy(tile).wait()
        term = jnp.dot(x_ref[...], buffer[tile % slots, :, :width], preferred_element_type=F32)
        if tile + slots < len(tiles):
            copy(tile + slots).start()
        if step == 1:
            place = pl.ds(array * share_width + offset, width)
            outs[-1][:, place] = term.astype(BF16)
        elif count == 3:
            outs[array][:, pl.ds(offset, width)] = term.astype(BF16)
        elif tile == 0:
            outs[0][: rows - 16, :] = term[: rows - 16].astype(BF16)
            outs[0][rows - 16 :, :] = coded(s_ref[0:1, :], term[rows - 16 :])
        else:
            outs[tile][...] = term.astype(BF16)


def gate_up(me, x, squares, w_gate, w_up, tp, cuts, mine, after):
    rows, feats = x.shape
    width = w_gate.shape[1] // tp
    shares = (1, 0) if mine else (3, 2)
    if width % 128:
        sums = [
            jnp.dot(x, w, preferred_element_type=F32).astype(BF16).reshape(rows, tp, width)
            for w in (w_gate, w_up)
        ]
        out = [
            [lax.dynamic_index_in_dim(p, me[0] ^ share, 1, False) for p in sums] for share in shares
        ]
        joined = [jnp.concatenate(pair, axis=1) for pair in out]
        if mine:
            return out[0] + joined[1:]
        return [coded(squares[0:1], out[0][0]), out[0][1], joined[1]]
    whole = ((rows, 2 * width), BF16)
    pieces = [((rows, w), BF16) for _ in range(2) for _, w in cuts]
    outs = [((rows, width), BF16)] * 2 if mine else pieces
    outs = outs + [whole]
    return call(
        functools.partial(
            gate_up_kernel, share_width=width, cuts=cuts, shares=shares, count=len(outs)
        ),
        outs,
        (me, x, squares, w_gate, w_up),
        [SMEM, VMEM, VMEM, HBM, HBM],
        f"gate_up_{rows}_{int(mine)}",
        50,
        scratch=[
            pltpu.VMEM((4, feats, max(w for _, w in cuts)), BF16),
            pltpu.SemaphoreType.DMA((4,)),
        ],
        after=after,
    )


def add_kernel(own_ref, s_ref, *refs, cuts, count):
    gots, (out_ref, sum_ref) = refs[:count], refs[-2:]
    rows, width = own_ref.shape
    for number, got in enumerate(gots):
        array, cut = divmod(number, len(cuts))
        offset, part = cuts[cut]
        place = pl.ds(array * (width // 2) + offset, part)
        total = own_ref[:, place].astype(F32) + got[...].astype(F32)
        out_ref[:, place] = total.astype(BF16)
    squares = s_ref[0:1, :] + decoded(gots[0][rows - 16 :, :])
    out_ref[rows - 16 :, :] = coded(squares, out_ref[rows - 16 :, :])
    sum_ref[...] = jnp.broadcast_to(squares, sum_ref.shape)


def add(own, gots, squares, cuts, after):
    return call(
        functools.partial(add_kernel, cuts=cuts, count=len(gots)),
        [(own.shape, BF16), ((8, LANES), F32)],
        (own, squares, *gots),
        [VMEM] * (2 + len(gots)),
        "add",
        16,
        after=after,
    )


def silu_kernel(a_ref, g_ref, u_ref, c_ref, s_ref, *refs, cuts):
    out_ref, pieces = refs[-1 - len(cuts)], refs[-len(cuts) :]
    rows, width = out_ref.shape
    squares = s_ref[0:1, :] + decoded(c_ref[rows - 16 :, :])
    row = lax.broadcasted_iota(jnp.int32, (rows, LANES), 0)
    lane = lax.broadcasted_iota(jnp.int32, (rows, LANES), 1)
    column = jnp.sum(jnp.where(row == lane, squares, 0.0), axis=1, keepdims=True)
    scale = jnp.where(row[:, :1] < rows - SPARE, lax.rsqrt(column / D + EPS), 0.0)

    def total(got, part):
        return (a_ref[:, part].astype(F32) + got[...].astype(F32) + c_ref[:, part].astype(F32)) * scale

    gate, up = total(g_ref, slice(0, width)), total(u_ref, slice(width, 2 * width))
    hidden = (gate / (1.0 + jnp.exp(-gate)) * up).astype(BF16)
    out_ref[...] = hidden
    for piece, (offset, part) in zip(pieces, cuts):
        piece[...] = hidden[:, offset : offset + part]


def silu(a, gate, up, c, squares, cuts, after):
    rows, width = a.shape
    return call(
        functools.partial(silu_kernel, cuts=cuts),
        [((rows, width // 2), BF16)] + [((rows, part), BF16) for _, part in cuts],
        (a, gate, up, c, squares),
        [VMEM] * 5,
        "silu",
        16,
        after=after,
    )


def relay_kernel(in_ref, *refs, cuts):
    whole, pieces = refs[-1 - len(cuts)], refs[-len(cuts) :]
    whole[...] = in_ref[...]
    for piece, (offset, width) in zip(pieces, cuts):
        piece[...] = in_ref[:, offset : offset + width]


def relay(value, cuts, after):
    rows, _ = value.shape
    return call(
        functools.partial(relay_kernel, cuts=cuts),
        [(value.shape, BF16)] + [((rows, width), BF16) for _, width in cuts],
        (value,),
        [VMEM],
        "relay",
        16,
        after=after,
    )


def down_kernel(me_ref, extras_ref, w_ref, *refs, tiles, sources, share_width, window, last):
    me = me_ref[0]
    if last:
        outs, acc, buffer = refs[-GROUP - 1 : -1], refs[-1], w_ref
    else:
        (out, ahead), (acc, buffer, sems) = refs[-5:-3], refs[-3:]

    def copy(tile, later):
        share, offset, depth, _, _ = tiles[tile]
        begin = pl.multiple_of((me ^ share ^ (2 * later)) * share_width + offset, 16)
        target = (ahead if later else buffer).at[tile, pl.ds(0, depth), :]
        sem = sems.at[later * len(tiles) + tile]
        return pltpu.make_async_copy(w_ref.at[pl.ds(begin, depth), :], target, sem)

    if not last:
        for later in range(2):
            for tile in range(len(tiles)):
                copy(tile, later).start()
    for tile, (_, _, depth, source, begin) in enumerate(tiles):
        if not last:
            copy(tile, 0).wait()
        hidden = refs[source][:, begin : begin + depth]
        term = jnp.dot(hidden, buffer[tile, :depth, :], preferred_element_type=F32)
        if tile == 0:
            acc[...] = refs[sources][...] + term if last else term
        else:
            acc[...] += term
    if not last:
        out[...] = acc[...]
        for tile in range(len(tiles)):
            copy(tile, 1).wait()
        return

    partial = acc[...].astype(BF16)
    rows = partial.shape[0]
    start = jnp.zeros((1, extras_ref.shape[1]), F32)
    for member, out in enumerate(outs):
        extras = extras_ref[member : member + 1, :]
        index = lax.broadcasted_iota(jnp.int32, (out.shape[0], rows), 0)
        slot = slots_of(index, extras[:, :rows], start[:, :rows], member, window)
        here = lax.broadcasted_iota(jnp.int32, (out.shape[0], rows), 1).astype(F32)
        hit = jnp.where(slot == here, 1.0, 0.0).astype(BF16)
        out[...] = jnp.dot(hit, partial, preferred_element_type=F32).astype(BF16)
        start = start + extras


def down(me, extras, w_down, hiddens, cuts, before, window, after):
    rows, width = hiddens[0].shape
    feats = w_down.shape[1]
    last = before is not None
    tiles = [(0, offset, depth, 0, offset) for offset, depth in cuts]
    for number, (offset, depth) in enumerate(cuts):
        source, begin = (number + 1, 0) if len(hiddens) > 2 else (1, offset)
        tiles.append((1, offset, depth, source, begin))
    held = pltpu.VMEM((len(tiles), max(depth for _, depth in cuts), feats), BF16)
    return call(
        functools.partial(
            down_kernel,
            tiles=tiles,
            sources=len(hiddens),
            share_width=width,
            window=window,
            last=last,
        ),
        [((SURE + window, feats), BF16)] * GROUP if last else [((rows, feats), F32), held],
        (me, extras, before[1] if last else w_down, *hiddens) + ((before[0],) if last else ()),
        [SMEM, VMEM, VMEM if last else HBM] + [VMEM] * (len(hiddens) + last),
        f"down_{rows}_{int(last)}",
        32,
        scratch=[pltpu.VMEM((rows, feats), F32)]
        + ([] if last else [held, pltpu.SemaphoreType.DMA((2 * len(tiles),))]),
        after=after,
    )


def gather_group(rows, n_ctx):
    return [rows] + [swap(rows, "ctx", n_ctx, j) for j in range(1, GROUP)]


def sum_kernel(a_ref, b_ref, c_ref, d_ref, *refs):
    total = a_ref[...].astype(F32) + b_ref[...].astype(F32)
    refs[-1][...] = (total + c_ref[...].astype(F32) + d_ref[...].astype(F32)).astype(BF16)


def reduce_group(blocks, n_ctx, after):
    got = [blocks[0]] + [swap(blocks[j], "ctx", n_ctx, j) for j in range(1, GROUP)]
    return call(
        sum_kernel, [(blocks[0].shape, BF16)], got, [VMEM] * GROUP, "sum", 16, after=after
    )[0]


def body(hidden_states, counts, selected, router_weight, norm_gain, w_gate, w_up, w_down, *, n_ctx, tp):
    me = lax.axis_index("tp").astype(jnp.int32).reshape(1)
    chosen = selected[0]
    most = chosen.shape[0]
    tokens, feats = hidden_states.shape
    window = most - SURE
    inner = min(2, n_ctx // GROUP - 1)
    slots = -(-(GROUP * (SEL - SURE) + SLACK * inner + SPARE) // 16) * 16
    height = GROUP * SURE + slots
    gain = norm_gain[None, :]
    share_width = w_gate.shape[1] // tp
    first = -(-share_width // 256) * 128
    cuts = [(0, share_width)]
    if share_width % 128 == 0 and first < share_width:
        cuts = [(0, first), (first, share_width - first)]

    rows = call(
        pick_kernel,
        [((most, feats), BF16)],
        (counts, selected, hidden_states),
        [SMEM, VMEM, VMEM],
        "pick",
        16,
    )[0]
    sources = [gather_group(rows, n_ctx)]
    for d in range(GROUP, n_ctx, GROUP):
        sources.append(gather_group(swap(rows, "ctx", n_ctx, d), n_ctx))
    weights = (w_gate, w_up, tp, cuts)

    chunks = [assemble(gain, members, height, window) for members in sources]
    begun, after = [], []
    for number, (x, squares, _) in enumerate(chunks):
        *sends, keep = gate_up(me, x, squares, *weights, False, after)
        gots = [swap(piece, "tp", tp, 1) for piece in sends]
        outgoing, two = add(keep, gots, squares, cuts, [] if number else chunks[1][:1])
        begun.append((swap(outgoing, "tp", tp, 2), two))
        after = [outgoing]
    owns, cores, parts = [], [], []
    for (x, squares, extras), (across, two) in zip(chunks, begun):
        *sends, keep = gate_up(me, x, squares, *weights, True, after)
        gots = [swap(piece, "tp", tp, 1) for piece in sends]
        own, *pieces = silu(keep, *gots, across, two, cuts, parts[0][:1] if parts else [])
        after = [own]
        owns.append(own)
        cores.append([swap(piece, "tp", tp, 1) for piece in pieces])
        if not parts:
            parts.append(down(me, extras, w_down, (own, *cores[0]), cuts, None, window, []))

    blocks, behind = [], []
    for number in [*range(1, len(chunks)), 0]:
        extras = chunks[number][2]
        other_y = swap(owns[number], "tp", tp, 2)
        if number:
            hidden = (owns[number], *cores[number])
            part = down(me, extras, w_down, hidden, cuts, None, window, behind)
        else:
            part = parts[0]
        other_y, *pieces = relay(other_y, cuts, part[:1] + behind)
        both = [swap(piece, "tp", tp, 1) for piece in pieces]
        blocks.append(down(me, extras, w_down, (other_y, *both), cuts, part, window, []))
        behind = blocks[-1][:1]

    total = 0.0
    for number, parts in enumerate(blocks[:-1]):
        summed = reduce_group(parts, n_ctx, blocks[-1][:1])
        total = total + swap(summed, "ctx", n_ctx, GROUP * (number + 1)).astype(F32)
    for number, part in enumerate(blocks[-1]):
        total = total + (swap(part, "ctx", n_ctx, number) if number else part).astype(F32)

    ffn = total.astype(BF16)
    active = jnp.arange(most, dtype=jnp.int32) < counts[0]
    place = jnp.arange(tokens, dtype=jnp.int32)
    put = ((chosen[None, :] == place[:, None]) & active[None, :]).astype(BF16)
    added = jnp.dot(put, ffn, preferred_element_type=F32) * router_weight[:, None]
    return (hidden_states.astype(F32) + added).astype(BF16)


def solution(mesh):
    placed = (
        P("ctx", "tp"),
        P("ctx"),
        P("ctx", None),
        P("ctx"),
        P("tp"),
        P("tp", "ctx"),
        P("tp", "ctx"),
        P("ctx", "tp"),
    )
    return jax.shard_map(
        functools.partial(body, n_ctx=mesh.shape["ctx"], tp=mesh.shape["tp"]),
        mesh=mesh,
        in_specs=placed,
        out_specs=P("ctx", "tp"),
        check_vma=False,
    )
```

```python
import functools

import jax
import jax.numpy as jnp
from jax import lax
from jax.experimental import pallas as pl
from jax.experimental.pallas import tpu as pltpu
from jax.sharding import PartitionSpec as P

D = 8192
SEL = 48
SURE = SEL // 2
SLACK = SEL // 4
GROUP = 4
EPS = 1e-05
NONE = 1024.0
MIB = 1 << 20
LANES = 256
SPARE = 3
F32 = jnp.float32
BF16 = jnp.bfloat16
VMEM = pl.BlockSpec(memory_space=pltpu.VMEM)
SMEM = pl.BlockSpec(memory_space=pltpu.SMEM)
HBM = pl.BlockSpec(memory_space=pltpu.HBM)
ANY = pl.BlockSpec(memory_space=pl.ANY)


def swap(value, axis, size, bit):
    return lax.ppermute(value, axis, [(i, i ^ bit) for i in range(size)])


def call(kernel, outs, operands, specs, name, limit, scratch=(), after=()):
    made = pl.pallas_call(
        kernel,
        out_shape=[
            jax.ShapeDtypeStruct(*out) if isinstance(out, tuple) else out for out in outs
        ],
        in_specs=list(specs) + [ANY] * len(after),
        out_specs=[VMEM] * len(outs),
        scratch_shapes=list(scratch),
        compiler_params=pltpu.CompilerParams(vmem_limit_bytes=limit * MIB),
        name=name,
    )(*operands, *after)
    return list(made)


def pick_kernel(count_ref, chosen_ref, tokens_ref, out_ref):
    tokens, most = tokens_ref.shape[0], out_ref.shape[0]
    place = lax.broadcasted_iota(jnp.int32, (tokens, most), 0)
    rows = lax.dot_general(
        jnp.where(chosen_ref[...] == place, 1.0, 0.0).astype(BF16),
        tokens_ref[...],
        (((0,), (0,)), ((), ())),
        preferred_element_type=F32,
    )
    index = lax.broadcasted_iota(jnp.int32, rows.shape, 0)
    out_ref[...] = jnp.where(index < count_ref[0], rows, NONE).astype(BF16)


def slots_of(index, extras, start, member, window):
    index = index.astype(F32)
    in_rest = index - SURE
    slot = jnp.where(index < SURE, index + member * SURE, in_rest + start + GROUP * SURE)
    valid = (index < SURE) | ((in_rest < extras) & (in_rest < window))
    return jnp.where(valid, slot, -1.0)


def assemble_kernel(gain_ref, *refs, window):
    sources, (x_ref, squares_ref, extras_ref) = refs[:GROUP], refs[-3:]
    rows, feats = x_ref.shape
    payload = sources[0].shape[0]
    lanes = extras_ref.shape[1]
    total = jnp.zeros((rows, feats), F32)
    start = jnp.zeros((1, lanes), F32)
    extras_ref[...] = jnp.zeros_like(extras_ref)
    for member, source in enumerate(sources):
        marks = source[:, :lanes].astype(F32)
        extras = jnp.sum(jnp.where(marks < NONE, 1.0, 0.0), axis=0, keepdims=True) - SURE
        extras_ref[member : member + 1, :] = extras
        index = lax.broadcasted_iota(jnp.int32, (rows, payload), 1)
        slot = slots_of(index, extras[:, :payload], start[:, :payload], member, window)
        here = lax.broadcasted_iota(jnp.int32, (rows, payload), 0).astype(F32)
        hit = jnp.where(slot == here, 1.0, 0.0).astype(BF16)
        total += jnp.dot(hit, source[...], preferred_element_type=F32)
        start = start + extras
    x_ref[...] = (total * gain_ref[...]).astype(BF16)
    sums = jnp.sum(total * total, axis=1, keepdims=True)
    row = lax.broadcasted_iota(jnp.int32, (rows, lanes), 0)
    lane = lax.broadcasted_iota(jnp.int32, (rows, lanes), 1)
    spread = jnp.sum(jnp.where(row == lane, sums, 0.0), axis=0, keepdims=True)
    squares_ref[...] = jnp.broadcast_to(spread, squares_ref.shape)


def assemble(gain, sources, rows, window, after=()):
    feats = sources[0].shape[1]
    return call(
        functools.partial(assemble_kernel, window=window),
        [((rows, feats), BF16), ((8, LANES), F32), ((8, LANES), F32)],
        (gain, *sources),
        [VMEM] * (1 + GROUP),
        f"assemble_{rows}",
        24,
        after=after,
    )


def coded(squares, block):
    high = squares.astype(BF16).astype(F32)
    middle = (squares - high).astype(BF16).astype(F32)
    width = block.shape[1]
    terms = []
    for term in (high, middle, squares - high - middle):
        if width > LANES:
            term = jnp.concatenate([term, jnp.zeros((1, width - LANES), F32)], axis=1)
        terms.append(term[:, :width])
    row = lax.broadcasted_iota(jnp.int32, block.shape, 0) - (block.shape[0] - SPARE)
    block = block.astype(F32)
    for number, term in enumerate(terms):
        block = jnp.where(row == number, term, block)
    return block.astype(BF16)


def decoded(block):
    block = block.astype(F32)
    total = block[13:14] + block[14:15] + block[15:16]
    if total.shape[1] < LANES:
        total = jnp.concatenate([total, jnp.zeros((1, LANES - total.shape[1]), F32)], axis=1)
    return total[:, :LANES]


def gate_up_kernel(
    me_ref, x_ref, s_ref, g_ref, u_ref, *refs, share_width, cuts, shares, count, code
):
    outs, (buffer, sems) = refs[-2 - count : -2], refs[-2:]
    me = me_ref[0]
    rows = x_ref.shape[0]
    slots = buffer.shape[0]
    tiles = [(step, array, cut) for step in range(2) for array in range(2) for cut in range(len(cuts))]

    def copy(tile):
        step, array, cut = tiles[tile]
        offset, width = cuts[cut]
        begin = pl.multiple_of((me ^ shares[step]) * share_width + offset, 128)
        source = (g_ref, u_ref)[array].at[:, pl.ds(begin, width)]
        slot = tile % slots
        return pltpu.make_async_copy(source, buffer.at[slot, :, pl.ds(0, width)], sems.at[slot])

    for tile in range(min(slots, len(tiles))):
        copy(tile).start()
    for tile, (step, array, cut) in enumerate(tiles):
        offset, width = cuts[cut]
        copy(tile).wait()
        term = jnp.dot(x_ref[...], buffer[tile % slots, :, :width], preferred_element_type=F32)
        if tile + slots < len(tiles):
            copy(tile + slots).start()
        if step == 1:
            place = pl.ds(array * share_width + offset, width)
            outs[-1][:, place] = term.astype(BF16)
        elif count == 3 and len(cuts) > 1:
            outs[array][:, pl.ds(offset, width)] = term.astype(BF16)
        elif tile == 0 and code:
            outs[0][: rows - 16, :] = term[: rows - 16].astype(BF16)
            outs[0][rows - 16 :, :] = coded(s_ref[0:1, :], term[rows - 16 :])
        else:
            outs[tile][...] = term.astype(BF16)


def gate_up(me, x, squares, w_gate, w_up, tp, cuts, mine, after, split=True):
    rows, feats = x.shape
    width = w_gate.shape[1] // tp
    shares = (1, 0) if mine else (3, 2)
    if width % 128:
        sums = [
            jnp.dot(x, w, preferred_element_type=F32).astype(BF16).reshape(rows, tp, width)
            for w in (w_gate, w_up)
        ]
        out = [
            [lax.dynamic_index_in_dim(p, me[0] ^ share, 1, False) for p in sums] for share in shares
        ]
        joined = [jnp.concatenate(pair, axis=1) for pair in out]
        if mine:
            return out[0] + joined[1:]
        return [coded(squares[0:1], out[0][0]), out[0][1], joined[1]]
    whole = ((rows, 2 * width), BF16)
    pieces = [((rows, w), BF16) for _ in range(2) for _, w in cuts]
    outs = pieces if split else [((rows, width), BF16)] * 2
    outs = outs + [whole]
    return call(
        functools.partial(
            gate_up_kernel,
            share_width=width,
            cuts=cuts,
            shares=shares,
            count=len(outs),
            code=not mine,
        ),
        outs,
        (me, x, squares, w_gate, w_up),
        [SMEM, VMEM, VMEM, HBM, HBM],
        f"gate_up_{rows}_{int(mine)}",
        50,
        scratch=[
            pltpu.VMEM((4, feats, max(w for _, w in cuts)), BF16),
            pltpu.SemaphoreType.DMA((4,)),
        ],
        after=after,
    )


def add_kernel(own_ref, s_ref, *refs, cuts, count):
    gots, (out_ref, sum_ref) = refs[:count], refs[-2:]
    rows, width = own_ref.shape
    for number, got in enumerate(gots):
        array, cut = divmod(number, len(cuts))
        offset, part = cuts[cut]
        place = pl.ds(array * (width // 2) + offset, part)
        total = own_ref[:, place].astype(F32) + got[...].astype(F32)
        out_ref[:, place] = total.astype(BF16)
    squares = s_ref[0:1, :] + decoded(gots[0][rows - 16 :, :])
    out_ref[rows - 16 :, :] = coded(squares, out_ref[rows - 16 :, :])
    sum_ref[...] = jnp.broadcast_to(squares, sum_ref.shape)


def add(own, gots, squares, cuts, after):
    return call(
        functools.partial(add_kernel, cuts=cuts, count=len(gots)),
        [(own.shape, BF16), ((8, LANES), F32)],
        (own, squares, *gots),
        [VMEM] * (2 + len(gots)),
        "add",
        16,
        after=after,
    )


def silu_kernel(a_ref, c_ref, s_ref, *refs, cuts, count):
    gots, out_ref, pieces = refs[:count], refs[-1 - len(cuts)], refs[-len(cuts) :]
    rows, width = out_ref.shape
    squares = s_ref[0:1, :] + decoded(c_ref[rows - 16 :, :])
    row = lax.broadcasted_iota(jnp.int32, (rows, LANES), 0)
    lane = lax.broadcasted_iota(jnp.int32, (rows, LANES), 1)
    column = jnp.sum(jnp.where(row == lane, squares, 0.0), axis=1, keepdims=True)
    scale = jnp.where(row[:, :1] < rows - SPARE, lax.rsqrt(column / D + EPS), 0.0)

    def total(array, cut):
        offset, part = cuts[cut]
        begin = array * width + offset
        if count == 2:
            got = gots[array][:, offset : offset + part]
        else:
            got = gots[array * len(cuts) + cut][...]
        a, c = a_ref[:, begin : begin + part], c_ref[:, begin : begin + part]
        return (a.astype(F32) + got.astype(F32) + c.astype(F32)) * scale

    for cut, (offset, part) in enumerate(cuts):
        gate, up = total(0, cut), total(1, cut)
        hidden = (gate / (1.0 + jnp.exp(-gate)) * up).astype(BF16)
        out_ref[:, offset : offset + part] = hidden
        pieces[cut][...] = hidden


def silu(a, gots, c, squares, cuts, after):
    rows, width = a.shape
    return call(
        functools.partial(silu_kernel, cuts=cuts, count=len(gots)),
        [((rows, width // 2), BF16)] + [((rows, part), BF16) for _, part in cuts],
        (a, c, squares, *gots),
        [VMEM] * (3 + len(gots)),
        "silu",
        16,
        after=after,
    )


def relay_kernel(in_ref, *refs, cuts):
    whole, *pieces = refs[-1 - len(cuts) :]
    whole[...] = in_ref[...]
    for piece, (offset, width) in zip(pieces, cuts):
        piece[...] = in_ref[:, offset : offset + width]


def relay(value, cuts, after):
    rows, _ = value.shape
    return call(
        functools.partial(relay_kernel, cuts=cuts),
        [(value.shape, BF16)] + [((rows, width), BF16) for _, width in cuts],
        (value,),
        [VMEM],
        "relay",
        16,
        after=after,
    )


def down_kernel(me_ref, extras_ref, w_ref, *refs, tiles, sources, share_width, window, last):
    me = me_ref[0]
    if last:
        outs, acc, buffer = refs[-GROUP - 1 : -1], refs[-1], w_ref
    else:
        (out, ahead), (acc, buffer, sems) = refs[-5:-3], refs[-3:]

    def copy(tile, later):
        share, offset, depth, _, _ = tiles[tile]
        begin = pl.multiple_of((me ^ share ^ (2 * later)) * share_width + offset, 16)
        target = (ahead if later else buffer).at[tile, pl.ds(0, depth), :]
        sem = sems.at[later * len(tiles) + tile]
        return pltpu.make_async_copy(w_ref.at[pl.ds(begin, depth), :], target, sem)

    if not last:
        for later in range(2):
            for tile in range(len(tiles)):
                copy(tile, later).start()
    for tile, (_, _, depth, source, begin) in enumerate(tiles):
        if not last:
            copy(tile, 0).wait()
        hidden = refs[source][:, begin : begin + depth]
        term = jnp.dot(hidden, buffer[tile, :depth, :], preferred_element_type=F32)
        if tile == 0:
            acc[...] = refs[sources][...] + term if last else term
        else:
            acc[...] += term
    if not last:
        out[...] = acc[...]
        for tile in range(len(tiles)):
            copy(tile, 1).wait()
        return

    partial = acc[...].astype(BF16)
    rows = partial.shape[0]
    start = jnp.zeros((1, extras_ref.shape[1]), F32)
    for member, out in enumerate(outs):
        extras = extras_ref[member : member + 1, :]
        index = lax.broadcasted_iota(jnp.int32, (out.shape[0], rows), 0)
        slot = slots_of(index, extras[:, :rows], start[:, :rows], member, window)
        here = lax.broadcasted_iota(jnp.int32, (out.shape[0], rows), 1).astype(F32)
        hit = jnp.where(slot == here, 1.0, 0.0).astype(BF16)
        out[...] = jnp.dot(hit, partial, preferred_element_type=F32).astype(BF16)
        start = start + extras


def down(me, extras, w_down, hiddens, cuts, before, window, after):
    rows, width = hiddens[0].shape
    feats = w_down.shape[1]
    last = before is not None
    tiles = [(0, offset, depth, 0, offset) for offset, depth in cuts]
    for number, (offset, depth) in enumerate(cuts):
        source, begin = (number + 1, 0) if len(hiddens) > 2 else (1, offset)
        tiles.append((1, offset, depth, source, begin))
    held = pltpu.VMEM((len(tiles), max(depth for _, depth in cuts), feats), BF16)
    return call(
        functools.partial(
            down_kernel,
            tiles=tiles,
            sources=len(hiddens),
            share_width=width,
            window=window,
            last=last,
        ),
        [((SURE + window, feats), BF16)] * GROUP if last else [((rows, feats), F32), held],
        (me, extras, before[1] if last else w_down, *hiddens) + ((before[0],) if last else ()),
        [SMEM, VMEM, VMEM if last else HBM] + [VMEM] * (len(hiddens) + last),
        f"down_{rows}_{int(last)}",
        32,
        scratch=[pltpu.VMEM((rows, feats), F32)]
        + ([] if last else [held, pltpu.SemaphoreType.DMA((2 * len(tiles),))]),
        after=after,
    )


def gather_group(rows, n_ctx):
    return [rows] + [swap(rows, "ctx", n_ctx, j) for j in range(1, GROUP)]


def sum_kernel(a_ref, b_ref, c_ref, d_ref, *refs):
    total = a_ref[...].astype(F32) + b_ref[...].astype(F32)
    refs[-1][...] = (total + c_ref[...].astype(F32) + d_ref[...].astype(F32)).astype(BF16)


def reduce_group(blocks, n_ctx, after):
    got = [blocks[0]] + [swap(blocks[j], "ctx", n_ctx, j) for j in range(1, GROUP)]
    return call(
        sum_kernel, [(blocks[0].shape, BF16)], got, [VMEM] * GROUP, "sum", 16, after=after
    )[0]


def body(hidden_states, counts, selected, router_weight, norm_gain, w_gate, w_up, w_down, *, n_ctx, tp):
    me = lax.axis_index("tp").astype(jnp.int32).reshape(1)
    chosen = selected[0]
    most = chosen.shape[0]
    tokens, feats = hidden_states.shape
    window = most - SURE
    inner = min(2, n_ctx // GROUP - 1)
    slots = -(-(GROUP * (SEL - SURE) + SLACK * inner + SPARE) // 16) * 16
    height = GROUP * SURE + slots
    gain = norm_gain[None, :]
    share_width = w_gate.shape[1] // tp
    first = -(-share_width // 256) * 128
    cuts = [(0, share_width)]
    if share_width % 128 == 0 and first < share_width:
        cuts = [(0, first), (first, share_width - first)]

    rows = call(
        pick_kernel,
        [((most, feats), BF16)],
        (counts, selected, hidden_states),
        [SMEM, VMEM, VMEM],
        "pick",
        16,
    )[0]
    sources = [gather_group(rows, n_ctx)]
    for d in range(GROUP, n_ctx, GROUP):
        sources.append(gather_group(swap(rows, "ctx", n_ctx, d), n_ctx))
    weights = (w_gate, w_up, tp, cuts)

    chunks = [assemble(gain, members, height, window) for members in sources]
    begun, after = [], []
    for number, (x, squares, _) in enumerate(chunks):
        *sends, keep = gate_up(me, x, squares, *weights, False, after)
        gots = [swap(piece, "tp", tp, 1) for piece in sends]
        outgoing, two = add(keep, gots, squares, cuts, [] if number else chunks[1][:1])
        begun.append((swap(outgoing, "tp", tp, 2), two))
        after = [outgoing]
    owns, cores, parts = [], [], []
    for (x, squares, extras), (across, two) in zip(chunks, begun):
        *sends, keep = gate_up(me, x, squares, *weights, True, after, not owns)
        gots = [swap(piece, "tp", tp, 1) for piece in sends]
        own, *pieces = silu(keep, gots, across, two, cuts, [])
        after = [own]
        owns.append(own)
        cores.append([swap(piece, "tp", tp, 1) for piece in pieces])
        if len(owns) == 2:
            extras = chunks[0][2]
            parts.append(down(me, extras, w_down, (owns[0], *cores[0]), cuts, None, window, [own]))

    blocks, behind = [], []
    for number in [*range(1, len(chunks)), 0]:
        extras = chunks[number][2]
        own = owns[number]
        if number:
            other_y = swap(own, "tp", tp, 2)
            hidden = (own, *cores[number])
            part = down(me, extras, w_down, hidden, cuts, None, window, behind)
            first = part[:1]
        else:
            other_y = swap(relay(own, [], first)[0], "tp", tp, 2)
            part = parts[0]
        other_y, *pieces = relay(other_y, cuts, part[:1] + behind)
        both = [swap(piece, "tp", tp, 1) for piece in pieces]
        blocks.append(down(me, extras, w_down, (other_y, *both), cuts, part, window, []))
        behind = blocks[-1][:1]

    total = 0.0
    for number, parts in enumerate(blocks[:-1]):
        summed = reduce_group(parts, n_ctx, blocks[-1][:1])
        total = total + swap(summed, "ctx", n_ctx, GROUP * (number + 1)).astype(F32)
    for number, part in enumerate(blocks[-1]):
        total = total + (swap(part, "ctx", n_ctx, number) if number else part).astype(F32)

    ffn = total.astype(BF16)
    active = jnp.arange(most, dtype=jnp.int32) < counts[0]
    place = jnp.arange(tokens, dtype=jnp.int32)
    put = ((chosen[None, :] == place[:, None]) & active[None, :]).astype(BF16)
    added = jnp.dot(put, ffn, preferred_element_type=F32) * router_weight[:, None]
    return (hidden_states.astype(F32) + added).astype(BF16)


def solution(mesh):
    placed = (
        P("ctx", "tp"),
        P("ctx"),
        P("ctx", None),
        P("ctx"),
        P("tp"),
        P("tp", "ctx"),
        P("tp", "ctx"),
        P("ctx", "tp"),
    )
    return jax.shard_map(
        functools.partial(body, n_ctx=mesh.shape["ctx"], tp=mesh.shape["tp"]),
        mesh=mesh,
        in_specs=placed,
        out_specs=P("ctx", "tp"),
        check_vma=False,
    )
```

```python
import functools

import jax
import jax.numpy as jnp
from jax import lax
from jax.experimental import pallas as pl
from jax.experimental.pallas import tpu as pltpu
from jax.sharding import PartitionSpec as P

D = 8192
SEL = 48
SURE = SEL // 2
SLACK = SEL // 4
GROUP = 4
ORDER = (2, 3, 1)
EPS = 1e-05
NONE = 1024.0
MIB = 1 << 20
LANES = 256
SPARE = 3
F32 = jnp.float32
BF16 = jnp.bfloat16
VMEM = pl.BlockSpec(memory_space=pltpu.VMEM)
SMEM = pl.BlockSpec(memory_space=pltpu.SMEM)
HBM = pl.BlockSpec(memory_space=pltpu.HBM)
ANY = pl.BlockSpec(memory_space=pl.ANY)


def swap(value, axis, size, bit):
    return lax.ppermute(value, axis, [(i, i ^ bit) for i in range(size)])


def call(kernel, outs, operands, specs, name, limit, scratch=(), after=()):
    made = pl.pallas_call(
        kernel,
        out_shape=[
            jax.ShapeDtypeStruct(*out) if isinstance(out, tuple) else out for out in outs
        ],
        in_specs=list(specs) + [ANY] * len(after),
        out_specs=[VMEM] * len(outs),
        scratch_shapes=list(scratch),
        compiler_params=pltpu.CompilerParams(vmem_limit_bytes=limit * MIB),
        name=name,
    )(*operands, *after)
    return list(made)


def pick_kernel(count_ref, chosen_ref, tokens_ref, out_ref):
    tokens, most = tokens_ref.shape[0], out_ref.shape[0]
    place = lax.broadcasted_iota(jnp.int32, (tokens, most), 0)
    rows = lax.dot_general(
        jnp.where(chosen_ref[...] == place, 1.0, 0.0).astype(BF16),
        tokens_ref[...],
        (((0,), (0,)), ((), ())),
        preferred_element_type=F32,
    )
    index = lax.broadcasted_iota(jnp.int32, rows.shape, 0)
    out_ref[...] = jnp.where(index < count_ref[0], rows, NONE).astype(BF16)


def slots_of(index, extras, start, member, window):
    index = index.astype(F32)
    in_rest = index - SURE
    slot = jnp.where(index < SURE, index + member * SURE, in_rest + start + GROUP * SURE)
    valid = (index < SURE) | ((in_rest < extras) & (in_rest < window))
    return jnp.where(valid, slot, -1.0)


def assemble_kernel(gain_ref, *refs, window):
    sources, (x_ref, squares_ref, extras_ref) = refs[:GROUP], refs[-3:]
    rows, feats = x_ref.shape
    payload = sources[0].shape[0]
    lanes = extras_ref.shape[1]
    total = jnp.zeros((rows, feats), F32)
    start = jnp.zeros((1, lanes), F32)
    extras_ref[...] = jnp.zeros_like(extras_ref)
    for member, source in enumerate(sources):
        marks = source[:, :lanes].astype(F32)
        extras = jnp.sum(jnp.where(marks < NONE, 1.0, 0.0), axis=0, keepdims=True) - SURE
        extras_ref[member : member + 1, :] = extras
        index = lax.broadcasted_iota(jnp.int32, (rows, payload), 1)
        slot = slots_of(index, extras[:, :payload], start[:, :payload], member, window)
        here = lax.broadcasted_iota(jnp.int32, (rows, payload), 0).astype(F32)
        hit = jnp.where(slot == here, 1.0, 0.0).astype(BF16)
        total += jnp.dot(hit, source[...], preferred_element_type=F32)
        start = start + extras
    x_ref[...] = (total * gain_ref[...]).astype(BF16)
    sums = jnp.sum(total * total, axis=1, keepdims=True)
    row = lax.broadcasted_iota(jnp.int32, (rows, lanes), 0)
    lane = lax.broadcasted_iota(jnp.int32, (rows, lanes), 1)
    spread = jnp.sum(jnp.where(row == lane, sums, 0.0), axis=0, keepdims=True)
    squares_ref[...] = jnp.broadcast_to(spread, squares_ref.shape)


def assemble(gain, sources, rows, window, after=()):
    feats = sources[0].shape[1]
    return call(
        functools.partial(assemble_kernel, window=window),
        [((rows, feats), BF16), ((8, LANES), F32), ((8, LANES), F32)],
        (gain, *sources),
        [VMEM] * (1 + GROUP),
        f"assemble_{rows}",
        24,
        after=after,
    )


def coded(squares, block):
    high = squares.astype(BF16).astype(F32)
    middle = (squares - high).astype(BF16).astype(F32)
    width = block.shape[1]
    terms = []
    for term in (high, middle, squares - high - middle):
        if width > LANES:
            term = jnp.concatenate([term, jnp.zeros((1, width - LANES), F32)], axis=1)
        terms.append(term[:, :width])
    row = lax.broadcasted_iota(jnp.int32, block.shape, 0) - (block.shape[0] - SPARE)
    block = block.astype(F32)
    for number, term in enumerate(terms):
        block = jnp.where(row == number, term, block)
    return block.astype(BF16)


def decoded(block):
    block = block.astype(F32)
    total = block[13:14] + block[14:15] + block[15:16]
    if total.shape[1] < LANES:
        total = jnp.concatenate([total, jnp.zeros((1, LANES - total.shape[1]), F32)], axis=1)
    return total[:, :LANES]


def gate_up_kernel(
    me_ref, x_ref, s_ref, g_ref, u_ref, *refs, share_width, cuts, shares, count, code
):
    outs, (buffer, sems) = refs[-2 - count : -2], refs[-2:]
    me = me_ref[0]
    rows = x_ref.shape[0]
    slots = buffer.shape[0]
    tiles = [(step, array, cut) for step in range(2) for array in range(2) for cut in range(len(cuts))]

    def copy(tile):
        step, array, cut = tiles[tile]
        offset, width = cuts[cut]
        begin = pl.multiple_of((me ^ shares[step]) * share_width + offset, 128)
        source = (g_ref, u_ref)[array].at[:, pl.ds(begin, width)]
        slot = tile % slots
        return pltpu.make_async_copy(source, buffer.at[slot, :, pl.ds(0, width)], sems.at[slot])

    for tile in range(min(slots, len(tiles))):
        copy(tile).start()
    for tile, (step, array, cut) in enumerate(tiles):
        offset, width = cuts[cut]
        copy(tile).wait()
        term = jnp.dot(x_ref[...], buffer[tile % slots, :, :width], preferred_element_type=F32)
        if tile + slots < len(tiles):
            copy(tile + slots).start()
        if step == 1:
            place = pl.ds(array * share_width + offset, width)
            outs[-1][:, place] = term.astype(BF16)
        elif count == 3 and len(cuts) > 1:
            outs[array][:, pl.ds(offset, width)] = term.astype(BF16)
        elif tile == 0 and code:
            outs[0][: rows - 16, :] = term[: rows - 16].astype(BF16)
            outs[0][rows - 16 :, :] = coded(s_ref[0:1, :], term[rows - 16 :])
        else:
            outs[tile][...] = term.astype(BF16)


def gate_up(me, x, squares, w_gate, w_up, tp, cuts, mine, after, split=True):
    rows, feats = x.shape
    width = w_gate.shape[1] // tp
    shares = (1, 0) if mine else (3, 2)
    if width % 128:
        sums = [
            jnp.dot(x, w, preferred_element_type=F32).astype(BF16).reshape(rows, tp, width)
            for w in (w_gate, w_up)
        ]
        out = [
            [lax.dynamic_index_in_dim(p, me[0] ^ share, 1, False) for p in sums] for share in shares
        ]
        joined = [jnp.concatenate(pair, axis=1) for pair in out]
        if mine:
            return out[0] + joined[1:]
        return [coded(squares[0:1], out[0][0]), out[0][1], joined[1]]
    whole = ((rows, 2 * width), BF16)
    pieces = [((rows, w), BF16) for _ in range(2) for _, w in cuts]
    outs = pieces if split else [((rows, width), BF16)] * 2
    outs = outs + [whole]
    return call(
        functools.partial(
            gate_up_kernel,
            share_width=width,
            cuts=cuts,
            shares=shares,
            count=len(outs),
            code=not mine,
        ),
        outs,
        (me, x, squares, w_gate, w_up),
        [SMEM, VMEM, VMEM, HBM, HBM],
        f"gate_up_{rows}_{int(mine)}",
        50,
        scratch=[
            pltpu.VMEM((4, feats, max(w for _, w in cuts)), BF16),
            pltpu.SemaphoreType.DMA((4,)),
        ],
        after=after,
    )


def add_kernel(own_ref, s_ref, *refs, cuts, count):
    gots, (out_ref, sum_ref) = refs[:count], refs[-2:]
    rows, width = own_ref.shape
    for number, got in enumerate(gots):
        array, cut = divmod(number, len(cuts))
        offset, part = cuts[cut]
        place = pl.ds(array * (width // 2) + offset, part)
        total = own_ref[:, place].astype(F32) + got[...].astype(F32)
        out_ref[:, place] = total.astype(BF16)
    squares = s_ref[0:1, :] + decoded(gots[0][rows - 16 :, :])
    out_ref[rows - 16 :, :] = coded(squares, out_ref[rows - 16 :, :])
    sum_ref[...] = jnp.broadcast_to(squares, sum_ref.shape)


def add(own, gots, squares, cuts, after):
    return call(
        functools.partial(add_kernel, cuts=cuts, count=len(gots)),
        [(own.shape, BF16), ((8, LANES), F32)],
        (own, squares, *gots),
        [VMEM] * (2 + len(gots)),
        "add",
        16,
        after=after,
    )


def silu_kernel(a_ref, c_ref, s_ref, *refs, cuts, count):
    gots, out_ref, pieces = refs[:count], refs[-1 - len(cuts)], refs[-len(cuts) :]
    rows, width = out_ref.shape
    squares = s_ref[0:1, :] + decoded(c_ref[rows - 16 :, :])
    row = lax.broadcasted_iota(jnp.int32, (rows, LANES), 0)
    lane = lax.broadcasted_iota(jnp.int32, (rows, LANES), 1)
    column = jnp.sum(jnp.where(row == lane, squares, 0.0), axis=1, keepdims=True)
    scale = jnp.where(row[:, :1] < rows - SPARE, lax.rsqrt(column / D + EPS), 0.0)

    def total(array, cut):
        offset, part = cuts[cut]
        begin = array * width + offset
        if count == 2:
            got = gots[array][:, offset : offset + part]
        else:
            got = gots[array * len(cuts) + cut][...]
        a, c = a_ref[:, begin : begin + part], c_ref[:, begin : begin + part]
        return (a.astype(F32) + got.astype(F32) + c.astype(F32)) * scale

    for cut, (offset, part) in enumerate(cuts):
        gate, up = total(0, cut), total(1, cut)
        hidden = (gate / (1.0 + jnp.exp(-gate)) * up).astype(BF16)
        out_ref[:, offset : offset + part] = hidden
        pieces[cut][...] = hidden


def silu(a, gots, c, squares, cuts, after):
    rows, width = a.shape
    return call(
        functools.partial(silu_kernel, cuts=cuts, count=len(gots)),
        [((rows, width // 2), BF16)] + [((rows, part), BF16) for _, part in cuts],
        (a, c, squares, *gots),
        [VMEM] * (3 + len(gots)),
        "silu",
        16,
        after=after,
    )


def relay_kernel(in_ref, *refs, cuts):
    whole, *pieces = refs[-1 - len(cuts) :]
    whole[...] = in_ref[...]
    for piece, (offset, width) in zip(pieces, cuts):
        piece[...] = in_ref[:, offset : offset + width]


def relay(value, cuts, after):
    rows, _ = value.shape
    return call(
        functools.partial(relay_kernel, cuts=cuts),
        [(value.shape, BF16)] + [((rows, width), BF16) for _, width in cuts],
        (value,),
        [VMEM],
        "relay",
        16,
        after=after,
    )


def down_kernel(me_ref, extras_ref, w_ref, *refs, tiles, sources, share_width, window, last):
    me = me_ref[0]
    if last:
        outs, acc, buffer = refs[-GROUP - 1 : -1], refs[-1], w_ref
    else:
        (out, ahead), (acc, buffer, sems) = refs[-5:-3], refs[-3:]

    def copy(tile, later):
        share, offset, depth, _, _ = tiles[tile]
        begin = pl.multiple_of((me ^ share ^ (2 * later)) * share_width + offset, 16)
        target = (ahead if later else buffer).at[tile, pl.ds(0, depth), :]
        sem = sems.at[later * len(tiles) + tile]
        return pltpu.make_async_copy(w_ref.at[pl.ds(begin, depth), :], target, sem)

    if not last:
        for later in range(2):
            for tile in range(len(tiles)):
                copy(tile, later).start()
    for tile, (_, _, depth, source, begin) in enumerate(tiles):
        if not last:
            copy(tile, 0).wait()
        hidden = refs[source][:, begin : begin + depth]
        term = jnp.dot(hidden, buffer[tile, :depth, :], preferred_element_type=F32)
        if tile == 0:
            acc[...] = refs[sources][...] + term if last else term
        else:
            acc[...] += term
    if not last:
        out[...] = acc[...]
        for tile in range(len(tiles)):
            copy(tile, 1).wait()
        return

    partial = acc[...].astype(BF16)
    rows = partial.shape[0]
    start = jnp.zeros((1, extras_ref.shape[1]), F32)
    for member, out in enumerate(outs):
        extras = extras_ref[member : member + 1, :]
        index = lax.broadcasted_iota(jnp.int32, (out.shape[0], rows), 0)
        slot = slots_of(index, extras[:, :rows], start[:, :rows], member, window)
        here = lax.broadcasted_iota(jnp.int32, (out.shape[0], rows), 1).astype(F32)
        hit = jnp.where(slot == here, 1.0, 0.0).astype(BF16)
        out[...] = jnp.dot(hit, partial, preferred_element_type=F32).astype(BF16)
        start = start + extras


def down(me, extras, w_down, hiddens, cuts, before, window, after):
    rows, width = hiddens[0].shape
    feats = w_down.shape[1]
    last = before is not None
    tiles = [(0, offset, depth, 0, offset) for offset, depth in cuts]
    for number, (offset, depth) in enumerate(cuts):
        source, begin = (number + 1, 0) if len(hiddens) > 2 else (1, offset)
        tiles.append((1, offset, depth, source, begin))
    held = pltpu.VMEM((len(tiles), max(depth for _, depth in cuts), feats), BF16)
    return call(
        functools.partial(
            down_kernel,
            tiles=tiles,
            sources=len(hiddens),
            share_width=width,
            window=window,
            last=last,
        ),
        [((SURE + window, feats), BF16)] * GROUP if last else [((rows, feats), F32), held],
        (me, extras, before[1] if last else w_down, *hiddens) + ((before[0],) if last else ()),
        [SMEM, VMEM, VMEM if last else HBM] + [VMEM] * (len(hiddens) + last),
        f"down_{rows}_{int(last)}",
        32,
        scratch=[pltpu.VMEM((rows, feats), F32)]
        + ([] if last else [held, pltpu.SemaphoreType.DMA((2 * len(tiles),))]),
        after=after,
    )


def gather_group(rows, n_ctx):
    return [rows] + [swap(rows, "ctx", n_ctx, j) for j in range(1, GROUP)]


def sum_kernel(a_ref, b_ref, c_ref, d_ref, *refs):
    total = a_ref[...].astype(F32) + b_ref[...].astype(F32)
    refs[-1][...] = (total + c_ref[...].astype(F32) + d_ref[...].astype(F32)).astype(BF16)


def reduce_group(blocks, n_ctx, after):
    got = [blocks[0]] + [swap(blocks[j], "ctx", n_ctx, j) for j in ORDER]
    return call(
        sum_kernel, [(blocks[0].shape, BF16)], got, [VMEM] * GROUP, "sum", 16, after=after
    )[0]


def body(hidden_states, counts, selected, router_weight, norm_gain, w_gate, w_up, w_down, *, n_ctx, tp):
    me = lax.axis_index("tp").astype(jnp.int32).reshape(1)
    chosen = selected[0]
    most = chosen.shape[0]
    tokens, feats = hidden_states.shape
    window = most - SURE
    inner = min(2, n_ctx // GROUP - 1)
    slots = -(-(GROUP * (SEL - SURE) + SLACK * inner + SPARE) // 16) * 16
    height = GROUP * SURE + slots
    gain = norm_gain[None, :]
    share_width = w_gate.shape[1] // tp
    first = -(-share_width // 256) * 128
    cuts = [(0, share_width)]
    if share_width % 128 == 0 and first < share_width:
        cuts = [(0, first), (first, share_width - first)]

    rows = call(
        pick_kernel,
        [((most, feats), BF16)],
        (counts, selected, hidden_states),
        [SMEM, VMEM, VMEM],
        "pick",
        16,
    )[0]
    sources = [gather_group(rows, n_ctx)]
    for d in range(GROUP, n_ctx, GROUP):
        sources.append(gather_group(swap(rows, "ctx", n_ctx, d), n_ctx))
    weights = (w_gate, w_up, tp, cuts)

    chunks = [assemble(gain, members, height, window) for members in sources]
    begun, after = [], []
    for number, (x, squares, _) in enumerate(chunks):
        *sends, keep = gate_up(me, x, squares, *weights, False, after)
        gots = [swap(piece, "tp", tp, 1) for piece in sends]
        outgoing, two = add(keep, gots, squares, cuts, [] if number else chunks[1][:1])
        begun.append((swap(outgoing, "tp", tp, 2), two))
        after = [outgoing]
    owns, cores, parts = [], [], []
    for (x, squares, extras), (across, two) in zip(chunks, begun):
        *sends, keep = gate_up(me, x, squares, *weights, True, after, not owns)
        gots = [swap(piece, "tp", tp, 1) for piece in sends]
        own, *pieces = silu(keep, gots, across, two, cuts, [])
        after = [own]
        owns.append(own)
        cores.append([swap(piece, "tp", tp, 1) for piece in pieces])
        if len(owns) == 2:
            extras = chunks[0][2]
            parts.append(down(me, extras, w_down, (owns[0], *cores[0]), cuts, None, window, [own]))

    blocks, behind = [], []
    for number in [*range(1, len(chunks)), 0]:
        extras = chunks[number][2]
        own = owns[number]
        if number:
            other_y = swap(own, "tp", tp, 2)
            hidden = (own, *cores[number])
            part = down(me, extras, w_down, hidden, cuts, None, window, behind)
            first = part[:1]
        else:
            other_y = swap(relay(own, [], first)[0], "tp", tp, 2)
            part = parts[0]
        other_y, *pieces = relay(other_y, cuts, part[:1] + behind)
        both = [swap(piece, "tp", tp, 1) for piece in pieces]
        blocks.append(down(me, extras, w_down, (other_y, *both), cuts, part, window, []))
        behind = blocks[-1][:1]

    total = 0.0
    for number, parts in enumerate(blocks[:-1]):
        summed = reduce_group(parts, n_ctx, [])
        total = total + swap(summed, "ctx", n_ctx, GROUP * (number + 1)).astype(F32)
    total = total + blocks[-1][0].astype(F32)
    for j in ORDER:
        total = total + swap(blocks[-1][j], "ctx", n_ctx, j).astype(F32)

    ffn = total.astype(BF16)
    active = jnp.arange(most, dtype=jnp.int32) < counts[0]
    place = jnp.arange(tokens, dtype=jnp.int32)
    put = ((chosen[None, :] == place[:, None]) & active[None, :]).astype(BF16)
    added = jnp.dot(put, ffn, preferred_element_type=F32) * router_weight[:, None]
    return (hidden_states.astype(F32) + added).astype(BF16)


def solution(mesh):
    placed = (
        P("ctx", "tp"),
        P("ctx"),
        P("ctx", None),
        P("ctx"),
        P("tp"),
        P("tp", "ctx"),
        P("tp", "ctx"),
        P("ctx", "tp"),
    )
    return jax.shard_map(
        functools.partial(body, n_ctx=mesh.shape["ctx"], tp=mesh.shape["tp"]),
        mesh=mesh,
        in_specs=placed,
        out_specs=P("ctx", "tp"),
        check_vma=False,
    )
```

```python
import functools

import jax
import jax.numpy as jnp
from jax import lax
from jax.experimental import pallas as pl
from jax.experimental.pallas import tpu as pltpu
from jax.sharding import PartitionSpec as P

D = 8192
SEL = 48
SURE = SEL // 2
SLACK = SEL // 4
GROUP = 4
ORDER = (3, 2, 1)
EPS = 1e-05
NONE = 1024.0
MIB = 1 << 20
LANES = 256
SPARE = 3
F32 = jnp.float32
BF16 = jnp.bfloat16
VMEM = pl.BlockSpec(memory_space=pltpu.VMEM)
SMEM = pl.BlockSpec(memory_space=pltpu.SMEM)
HBM = pl.BlockSpec(memory_space=pltpu.HBM)
ANY = pl.BlockSpec(memory_space=pl.ANY)


def swap(value, axis, size, bit):
    return lax.ppermute(value, axis, [(i, i ^ bit) for i in range(size)])


def call(kernel, outs, operands, specs, name, limit, scratch=(), after=()):
    made = pl.pallas_call(
        kernel,
        out_shape=[
            jax.ShapeDtypeStruct(*out) if isinstance(out, tuple) else out for out in outs
        ],
        in_specs=list(specs) + [ANY] * len(after),
        out_specs=[VMEM] * len(outs),
        scratch_shapes=list(scratch),
        compiler_params=pltpu.CompilerParams(vmem_limit_bytes=limit * MIB),
        name=name,
    )(*operands, *after)
    return list(made)


def pick_kernel(count_ref, chosen_ref, tokens_ref, out_ref):
    tokens, most = tokens_ref.shape[0], out_ref.shape[0]
    place = lax.broadcasted_iota(jnp.int32, (tokens, most), 0)
    rows = lax.dot_general(
        jnp.where(chosen_ref[...] == place, 1.0, 0.0).astype(BF16),
        tokens_ref[...],
        (((0,), (0,)), ((), ())),
        preferred_element_type=F32,
    )
    index = lax.broadcasted_iota(jnp.int32, rows.shape, 0)
    out_ref[...] = jnp.where(index < count_ref[0], rows, NONE).astype(BF16)


def slots_of(index, extras, start, member, window):
    index = index.astype(F32)
    in_rest = index - SURE
    slot = jnp.where(index < SURE, index + member * SURE, in_rest + start + GROUP * SURE)
    valid = (index < SURE) | ((in_rest < extras) & (in_rest < window))
    return jnp.where(valid, slot, -1.0)


def assemble_kernel(gain_ref, *refs, window):
    sources, (x_ref, squares_ref, extras_ref) = refs[:GROUP], refs[-3:]
    rows, feats = x_ref.shape
    payload = sources[0].shape[0]
    lanes = extras_ref.shape[1]
    total = jnp.zeros((rows, feats), F32)
    start = jnp.zeros((1, lanes), F32)
    extras_ref[...] = jnp.zeros_like(extras_ref)
    for member, source in enumerate(sources):
        marks = source[:, :lanes].astype(F32)
        extras = jnp.sum(jnp.where(marks < NONE, 1.0, 0.0), axis=0, keepdims=True) - SURE
        extras_ref[member : member + 1, :] = extras
        index = lax.broadcasted_iota(jnp.int32, (rows, payload), 1)
        slot = slots_of(index, extras[:, :payload], start[:, :payload], member, window)
        here = lax.broadcasted_iota(jnp.int32, (rows, payload), 0).astype(F32)
        hit = jnp.where(slot == here, 1.0, 0.0).astype(BF16)
        total += jnp.dot(hit, source[...], preferred_element_type=F32)
        start = start + extras
    x_ref[...] = (total * gain_ref[...]).astype(BF16)
    sums = jnp.sum(total * total, axis=1, keepdims=True)
    row = lax.broadcasted_iota(jnp.int32, (rows, lanes), 0)
    lane = lax.broadcasted_iota(jnp.int32, (rows, lanes), 1)
    spread = jnp.sum(jnp.where(row == lane, sums, 0.0), axis=0, keepdims=True)
    squares_ref[...] = jnp.broadcast_to(spread, squares_ref.shape)


def assemble(gain, sources, rows, window, after=()):
    feats = sources[0].shape[1]
    return call(
        functools.partial(assemble_kernel, window=window),
        [((rows, feats), BF16), ((8, LANES), F32), ((8, LANES), F32)],
        (gain, *sources),
        [VMEM] * (1 + GROUP),
        f"assemble_{rows}",
        24,
        after=after,
    )


def coded(squares, block):
    high = squares.astype(BF16).astype(F32)
    middle = (squares - high).astype(BF16).astype(F32)
    width = block.shape[1]
    terms = []
    for term in (high, middle, squares - high - middle):
        if width > LANES:
            term = jnp.concatenate([term, jnp.zeros((1, width - LANES), F32)], axis=1)
        terms.append(term[:, :width])
    row = lax.broadcasted_iota(jnp.int32, block.shape, 0) - (block.shape[0] - SPARE)
    block = block.astype(F32)
    for number, term in enumerate(terms):
        block = jnp.where(row == number, term, block)
    return block.astype(BF16)


def decoded(block):
    block = block.astype(F32)
    total = block[13:14] + block[14:15] + block[15:16]
    if total.shape[1] < LANES:
        total = jnp.concatenate([total, jnp.zeros((1, LANES - total.shape[1]), F32)], axis=1)
    return total[:, :LANES]


def gate_up_kernel(
    me_ref, x_ref, s_ref, g_ref, u_ref, *refs, share_width, cuts, shares, count, code
):
    outs, (buffer, sems) = refs[-2 - count : -2], refs[-2:]
    me = me_ref[0]
    rows = x_ref.shape[0]
    slots = buffer.shape[0]
    tiles = [(step, array, cut) for step in range(2) for array in range(2) for cut in range(len(cuts))]

    def copy(tile):
        step, array, cut = tiles[tile]
        offset, width = cuts[cut]
        begin = pl.multiple_of((me ^ shares[step]) * share_width + offset, 128)
        source = (g_ref, u_ref)[array].at[:, pl.ds(begin, width)]
        slot = tile % slots
        return pltpu.make_async_copy(source, buffer.at[slot, :, pl.ds(0, width)], sems.at[slot])

    for tile in range(min(slots, len(tiles))):
        copy(tile).start()
    for tile, (step, array, cut) in enumerate(tiles):
        offset, width = cuts[cut]
        copy(tile).wait()
        term = jnp.dot(x_ref[...], buffer[tile % slots, :, :width], preferred_element_type=F32)
        if tile + slots < len(tiles):
            copy(tile + slots).start()
        if step == 1:
            place = pl.ds(array * share_width + offset, width)
            outs[-1][:, place] = term.astype(BF16)
        elif count == 3 and len(cuts) > 1:
            outs[array][:, pl.ds(offset, width)] = term.astype(BF16)
        elif tile == 0 and code:
            outs[0][: rows - 16, :] = term[: rows - 16].astype(BF16)
            outs[0][rows - 16 :, :] = coded(s_ref[0:1, :], term[rows - 16 :])
        else:
            outs[tile][...] = term.astype(BF16)


def gate_up(me, x, squares, w_gate, w_up, tp, cuts, mine, after, split=True):
    rows, feats = x.shape
    width = w_gate.shape[1] // tp
    shares = (1, 0) if mine else (3, 2)
    if width % 128:
        sums = [
            jnp.dot(x, w, preferred_element_type=F32).astype(BF16).reshape(rows, tp, width)
            for w in (w_gate, w_up)
        ]
        out = [
            [lax.dynamic_index_in_dim(p, me[0] ^ share, 1, False) for p in sums] for share in shares
        ]
        joined = [jnp.concatenate(pair, axis=1) for pair in out]
        if mine:
            return out[0] + joined[1:]
        return [coded(squares[0:1], out[0][0]), out[0][1], joined[1]]
    whole = ((rows, 2 * width), BF16)
    pieces = [((rows, w), BF16) for _ in range(2) for _, w in cuts]
    outs = pieces if split else [((rows, width), BF16)] * 2
    outs = outs + [whole]
    return call(
        functools.partial(
            gate_up_kernel,
            share_width=width,
            cuts=cuts,
            shares=shares,
            count=len(outs),
            code=not mine,
        ),
        outs,
        (me, x, squares, w_gate, w_up),
        [SMEM, VMEM, VMEM, HBM, HBM],
        f"gate_up_{rows}_{int(mine)}",
        50,
        scratch=[
            pltpu.VMEM((4, feats, max(w for _, w in cuts)), BF16),
            pltpu.SemaphoreType.DMA((4,)),
        ],
        after=after,
    )


def add_kernel(own_ref, s_ref, *refs, cuts, count):
    gots, (out_ref, sum_ref) = refs[:count], refs[-2:]
    rows, width = own_ref.shape
    for number, got in enumerate(gots):
        array, cut = divmod(number, len(cuts))
        offset, part = cuts[cut]
        place = pl.ds(array * (width // 2) + offset, part)
        total = own_ref[:, place].astype(F32) + got[...].astype(F32)
        out_ref[:, place] = total.astype(BF16)
    squares = s_ref[0:1, :] + decoded(gots[0][rows - 16 :, :])
    out_ref[rows - 16 :, :] = coded(squares, out_ref[rows - 16 :, :])
    sum_ref[...] = jnp.broadcast_to(squares, sum_ref.shape)


def add(own, gots, squares, cuts, after):
    return call(
        functools.partial(add_kernel, cuts=cuts, count=len(gots)),
        [(own.shape, BF16), ((8, LANES), F32)],
        (own, squares, *gots),
        [VMEM] * (2 + len(gots)),
        "add",
        16,
        after=after,
    )


def silu_kernel(a_ref, c_ref, s_ref, *refs, cuts, count):
    gots, out_ref, pieces = refs[:count], refs[-1 - len(cuts)], refs[-len(cuts) :]
    rows, width = out_ref.shape
    squares = s_ref[0:1, :] + decoded(c_ref[rows - 16 :, :])
    row = lax.broadcasted_iota(jnp.int32, (rows, LANES), 0)
    lane = lax.broadcasted_iota(jnp.int32, (rows, LANES), 1)
    column = jnp.sum(jnp.where(row == lane, squares, 0.0), axis=1, keepdims=True)
    scale = jnp.where(row[:, :1] < rows - SPARE, lax.rsqrt(column / D + EPS), 0.0)

    def total(array, cut):
        offset, part = cuts[cut]
        begin = array * width + offset
        if count == 2:
            got = gots[array][:, offset : offset + part]
        else:
            got = gots[array * len(cuts) + cut][...]
        a, c = a_ref[:, begin : begin + part], c_ref[:, begin : begin + part]
        return (a.astype(F32) + got.astype(F32) + c.astype(F32)) * scale

    for cut, (offset, part) in enumerate(cuts):
        gate, up = total(0, cut), total(1, cut)
        hidden = (gate / (1.0 + jnp.exp(-gate)) * up).astype(BF16)
        out_ref[:, offset : offset + part] = hidden
        pieces[cut][...] = hidden


def silu(a, gots, c, squares, cuts, after):
    rows, width = a.shape
    return call(
        functools.partial(silu_kernel, cuts=cuts, count=len(gots)),
        [((rows, width // 2), BF16)] + [((rows, part), BF16) for _, part in cuts],
        (a, c, squares, *gots),
        [VMEM] * (3 + len(gots)),
        "silu",
        16,
        after=after,
    )


def relay_kernel(in_ref, *refs, cuts):
    whole, *pieces = refs[-1 - len(cuts) :]
    whole[...] = in_ref[...]
    for piece, (offset, width) in zip(pieces, cuts):
        piece[...] = in_ref[:, offset : offset + width]


def relay(value, cuts, after):
    rows, _ = value.shape
    return call(
        functools.partial(relay_kernel, cuts=cuts),
        [(value.shape, BF16)] + [((rows, width), BF16) for _, width in cuts],
        (value,),
        [VMEM],
        "relay",
        16,
        after=after,
    )


def down_kernel(me_ref, extras_ref, w_ref, *refs, tiles, sources, share_width, window, last):
    me = me_ref[0]
    if last:
        outs, acc, buffer = refs[-GROUP - 1 : -1], refs[-1], w_ref
    else:
        (out, ahead), (acc, buffer, sems) = refs[-5:-3], refs[-3:]

    def copy(tile, later):
        share, offset, depth, _, _ = tiles[tile]
        begin = pl.multiple_of((me ^ share ^ (2 * later)) * share_width + offset, 16)
        target = (ahead if later else buffer).at[tile, pl.ds(0, depth), :]
        sem = sems.at[later * len(tiles) + tile]
        return pltpu.make_async_copy(w_ref.at[pl.ds(begin, depth), :], target, sem)

    if not last:
        for later in range(2):
            for tile in range(len(tiles)):
                copy(tile, later).start()
    for tile, (_, _, depth, source, begin) in enumerate(tiles):
        if not last:
            copy(tile, 0).wait()
        hidden = refs[source][:, begin : begin + depth]
        term = jnp.dot(hidden, buffer[tile, :depth, :], preferred_element_type=F32)
        if tile == 0:
            acc[...] = refs[sources][...] + term if last else term
        else:
            acc[...] += term
    if not last:
        out[...] = acc[...]
        for tile in range(len(tiles)):
            copy(tile, 1).wait()
        return

    partial = acc[...].astype(BF16)
    rows = partial.shape[0]
    start = jnp.zeros((1, extras_ref.shape[1]), F32)
    for member, out in enumerate(outs):
        extras = extras_ref[member : member + 1, :]
        index = lax.broadcasted_iota(jnp.int32, (out.shape[0], rows), 0)
        slot = slots_of(index, extras[:, :rows], start[:, :rows], member, window)
        here = lax.broadcasted_iota(jnp.int32, (out.shape[0], rows), 1).astype(F32)
        hit = jnp.where(slot == here, 1.0, 0.0).astype(BF16)
        out[...] = jnp.dot(hit, partial, preferred_element_type=F32).astype(BF16)
        start = start + extras


def down(me, extras, w_down, hiddens, cuts, before, window, after):
    rows, width = hiddens[0].shape
    feats = w_down.shape[1]
    last = before is not None
    tiles = [(0, offset, depth, 0, offset) for offset, depth in cuts]
    for number, (offset, depth) in enumerate(cuts):
        source, begin = (number + 1, 0) if len(hiddens) > 2 else (1, offset)
        tiles.append((1, offset, depth, source, begin))
    held = pltpu.VMEM((len(tiles), max(depth for _, depth in cuts), feats), BF16)
    return call(
        functools.partial(
            down_kernel,
            tiles=tiles,
            sources=len(hiddens),
            share_width=width,
            window=window,
            last=last,
        ),
        [((SURE + window, feats), BF16)] * GROUP if last else [((rows, feats), F32), held],
        (me, extras, before[1] if last else w_down, *hiddens) + ((before[0],) if last else ()),
        [SMEM, VMEM, VMEM if last else HBM] + [VMEM] * (len(hiddens) + last),
        f"down_{rows}_{int(last)}",
        32,
        scratch=[pltpu.VMEM((rows, feats), F32)]
        + ([] if last else [held, pltpu.SemaphoreType.DMA((2 * len(tiles),))]),
        after=after,
    )


def gather_group(rows, n_ctx):
    return [rows] + [swap(rows, "ctx", n_ctx, j) for j in range(1, GROUP)]


def sum_kernel(a_ref, b_ref, c_ref, d_ref, *refs):
    total = a_ref[...].astype(F32) + b_ref[...].astype(F32)
    refs[-1][...] = (total + c_ref[...].astype(F32) + d_ref[...].astype(F32)).astype(BF16)


def reduce_group(blocks, n_ctx, after):
    got = [blocks[0]] + [swap(blocks[j], "ctx", n_ctx, j) for j in ORDER]
    return call(
        sum_kernel, [(blocks[0].shape, BF16)], got, [VMEM] * GROUP, "sum", 16, after=after
    )[0]


def body(hidden_states, counts, selected, router_weight, norm_gain, w_gate, w_up, w_down, *, n_ctx, tp):
    me = lax.axis_index("tp").astype(jnp.int32).reshape(1)
    chosen = selected[0]
    most = chosen.shape[0]
    tokens, feats = hidden_states.shape
    window = most - SURE
    inner = min(2, n_ctx // GROUP - 1)
    slots = -(-(GROUP * (SEL - SURE) + SLACK * inner + SPARE) // 16) * 16
    height = GROUP * SURE + slots
    gain = norm_gain[None, :]
    share_width = w_gate.shape[1] // tp
    first = -(-share_width // 256) * 128
    cuts = [(0, share_width)]
    if share_width % 128 == 0 and first < share_width:
        cuts = [(0, first), (first, share_width - first)]

    rows = call(
        pick_kernel,
        [((most, feats), BF16)],
        (counts, selected, hidden_states),
        [SMEM, VMEM, VMEM],
        "pick",
        16,
    )[0]
    sources = [gather_group(rows, n_ctx)]
    for d in range(GROUP, n_ctx, GROUP):
        sources.append(gather_group(swap(rows, "ctx", n_ctx, d), n_ctx))
    weights = (w_gate, w_up, tp, cuts)

    chunks = [assemble(gain, members, height, window) for members in sources]
    begun, after = [], []
    for number, (x, squares, _) in enumerate(chunks):
        *sends, keep = gate_up(me, x, squares, *weights, False, after)
        gots = [swap(piece, "tp", tp, 1) for piece in sends]
        outgoing, two = add(keep, gots, squares, cuts, [] if number else chunks[1][:1])
        begun.append((swap(outgoing, "tp", tp, 2), two))
        after = [outgoing]
    owns, cores, parts = [], [], []
    for (x, squares, extras), (across, two) in zip(chunks, begun):
        *sends, keep = gate_up(me, x, squares, *weights, True, after, not owns)
        gots = [swap(piece, "tp", tp, 1) for piece in sends]
        own, *pieces = silu(keep, gots, across, two, cuts, [])
        after = [own]
        owns.append(own)
        cores.append([swap(piece, "tp", tp, 1) for piece in pieces])
        if len(owns) == 2:
            extras = chunks[0][2]
            parts.append(down(me, extras, w_down, (owns[0], *cores[0]), cuts, None, window, [own]))

    blocks, behind = [], []
    for number in [*range(1, len(chunks)), 0]:
        extras = chunks[number][2]
        own = owns[number]
        if number:
            other_y = swap(own, "tp", tp, 2)
            hidden = (own, *cores[number])
            part = down(me, extras, w_down, hidden, cuts, None, window, behind)
            first = part[:1]
        else:
            other_y = swap(relay(own, [], first)[0], "tp", tp, 2)
            part = parts[0]
        other_y, *pieces = relay(other_y, cuts, part[:1] + behind)
        both = [swap(piece, "tp", tp, 1) for piece in pieces]
        blocks.append(down(me, extras, w_down, (other_y, *both), cuts, part, window, []))
        behind = blocks[-1][:1]

    total = 0.0
    for number, parts in enumerate(blocks[:-1]):
        summed = reduce_group(parts, n_ctx, [])
        total = total + swap(summed, "ctx", n_ctx, GROUP * (number + 1)).astype(F32)
    total = total + blocks[-1][0].astype(F32)
    for j in ORDER:
        total = total + swap(blocks[-1][j], "ctx", n_ctx, j).astype(F32)

    ffn = total.astype(BF16)
    active = jnp.arange(most, dtype=jnp.int32) < counts[0]
    place = jnp.arange(tokens, dtype=jnp.int32)
    put = ((chosen[None, :] == place[:, None]) & active[None, :]).astype(BF16)
    added = jnp.dot(put, ffn, preferred_element_type=F32) * router_weight[:, None]
    return (hidden_states.astype(F32) + added).astype(BF16)


def solution(mesh):
    placed = (
        P("ctx", "tp"),
        P("ctx"),
        P("ctx", None),
        P("ctx"),
        P("tp"),
        P("tp", "ctx"),
        P("tp", "ctx"),
        P("ctx", "tp"),
    )
    return jax.shard_map(
        functools.partial(body, n_ctx=mesh.shape["ctx"], tp=mesh.shape["tp"]),
        mesh=mesh,
        in_specs=placed,
        out_specs=P("ctx", "tp"),
        check_vma=False,
    )
```
